512 devices in a mesh: row: 32 (over x, z_lo, core), col: 16 (over y, z_hi).
Axes of the slice: x: 4, y: 4, z: 16 (z_hi: 4, z_lo: 4; z = z_hi * 4 + z_lo), core: 2. Of those that a mesh axis runs over, the one named last changes fastest.
Arguments:
- features: bfloat16 [65536, 256], P(('col', 'row')), may hold values from -6 to 6
- adjacency: bfloat16 [32, 16, 32, 128, 128], P('row', 'col'), may hold values from 0 to 0.109375, as said below
- block_rows: int32 [32, 16, 32], P('row', 'col'), may hold values from 0 to 15, as said below
- block_cols: int32 [32, 16, 32], P('row', 'col'), may hold values from 0 to 31
- block_count: int32 [32, 16], P('row', 'col'), may hold values from 1 to 32, as said below
- weight: bfloat16 [256, 256], replicated, may hold values from -3 to 3
- bias_term: float32 [256], replicated, may hold values from -3 to 3
- cotangent: bfloat16 [65536, 256], P(('row', 'col')), may hold values from -6 to 6
Outputs:
- hidden_out: bfloat16 [65536, 256], P(('row', 'col'))
- grad_weight: float32 [256, 256], replicated
- grad_bias: float32 [256], replicated
- grad_features: bfloat16 [65536, 256], P(('col', 'row'))
The draws below stay inside these ranges and needn't reach their ends.
Inputs may be any that keep to these rules, and one draw needn't show every extreme that they name: `adjacency`: tiles are sparse with nonnegative entries. Within one grid cell the 32 slots name distinct pairs (block_rows, block_cols). The live slots of a cell are its first block_count slots; some cell is full.
All inputs are finite; a program needn't handle non-finite values.
Results may differ from the reference program's by a relative error of at most 0.02.
Values may be sent and summed in bfloat16 or wider, within the bound.
A program may use at most 64 MiB of HBM per device.

```python
import math
import jax
import jax.numpy as jnp
from jax import lax

H = 256
BS = 128
SLAB_R = 2048
SLAB_C = 4096
RB = 16
CB = 32
MAXBLK = 32
DEGREE = 64
NODES = 65536
N_ROW = 32
N_COL = 16


def slot_positions(key):
    keys = jax.random.split(key, N_ROW * N_COL)

    def one_order(single_key):
        return jax.random.permutation(single_key, RB * CB)
    orders = jax.vmap(one_order)(keys)
    return orders[:, :MAXBLK].reshape(N_ROW, N_COL, MAXBLK).astype(jnp.int32)


def draw_block_rows(key, part):
    positions = slot_positions(key)
    return (positions // CB).astype(jnp.int32)


def draw_block_cols(key, part):
    positions = slot_positions(key)
    return (positions % CB).astype(jnp.int32)


def draw_block_count(key, part):
    key = jax.random.fold_in(key, 7)
    key_level, key_jitter, key_full = jax.random.split(key, 3)
    levels = jax.random.randint(key_level, (N_ROW * N_COL,), 0, 4)
    base_count = jnp.right_shift(jnp.full((N_ROW * N_COL,), MAXBLK, jnp.int32), levels.astype(jnp.int32))
    jitter = jax.random.randint(key_jitter, (N_ROW * N_COL,), 0, 4)
    counts = jnp.maximum(base_count - jitter, 1)
    chosen_cell = jax.random.randint(key_full, (), 0, N_ROW * N_COL)
    counts = counts.at[chosen_cell].set(MAXBLK)
    counts = jnp.minimum(counts, MAXBLK)
    return counts.reshape(N_ROW, N_COL).astype(jnp.int32)


def draw_adjacency(key, part):
    key = jax.random.fold_in(key, 11)
    key_mask, key_value, key_row, key_col = jax.random.split(key, 4)
    shape = (N_ROW, N_COL, MAXBLK, BS, BS)
    present = jax.random.uniform(key_mask, shape, jnp.float32) < 4.0 / BS
    values = jax.random.uniform(key_value, shape, jnp.float32, 0.5, 1.5)
    spread = math.log(2.0)
    row_scale = jnp.exp(jax.random.uniform(key_row, (N_ROW, N_COL, MAXBLK, BS, 1), jnp.float32, -spread, spread))
    col_scale = jnp.exp(jax.random.uniform(key_col, (N_ROW, N_COL, MAXBLK, 1, BS), jnp.float32, -spread, spread))
    entries = jnp.where(present, values * row_scale * col_scale / DEGREE, 0.0)
    return entries.astype(jnp.bfloat16)


def steps_of(own_key, shape, shards, least, top_value):
    factor_of = 1.0
    for position, shards_of in shards:
        steps = jax.random.uniform(jax.random.fold_in(jax.random.fold_in(own_key, 6), position), (shards_of,), jnp.float32, least / len(shards), top_value / len(shards))
        factor_of = factor_of * jnp.repeat(jnp.exp(steps), shape[position] // shards_of).reshape((-1,) + (1,) * (len(shape) - 1 - position))
    return factor_of


def scatter_about(stream_key, shape, deviation, reach, cuts=(), held_as=jnp.bfloat16):
    array = deviation * jax.random.normal(stream_key, shape, jnp.float32)
    if cuts:
        array = array * steps_of(stream_key, shape, cuts, -0.22, 0.18)
    return jnp.clip(array, -reach, reach).astype(held_as)


def setup_inputs(seed: int = 0) -> dict:
    key_list = jax.random.split(jax.random.key(seed), 9)
    return {
        "features": scatter_about(key_list[0], (NODES, H), 1.0, 6.0, ((0, 512),)),
        "adjacency": draw_adjacency(jax.random.fold_in(key_list[8], 71), 0),
        "block_rows": draw_block_rows(jax.random.fold_in(key_list[8], 71), 0),
        "block_cols": draw_block_cols(jax.random.fold_in(key_list[8], 71), 0),
        "block_count": draw_block_count(jax.random.fold_in(key_list[8], 71), 0),
        "weight": scatter_about(key_list[5], (H, H), (max(1, H // DEGREE)) ** -0.5, 3.0),
        "bias_term": scatter_about(key_list[6], (H,), 0.5, 3.0, (), jnp.float32),
        "cotangent": scatter_about(key_list[7], (NODES, H), 1.0, 6.0, ((0, 512),)),
    }


def gelu_exact(values):
    return jax.nn.gelu(values, approximate=False)

def block_sum(tile_set, source_blocks, source_ids, target_ids, is_live, target_count, transposed):
    chosen = jnp.take(source_blocks, source_ids, axis=0).astype(jnp.float32)
    tile_values = tile_set.astype(jnp.float32)
    if transposed:
        products = jnp.einsum('gji,gjh->gih', tile_values, chosen)
    else:
        products = jnp.einsum('gij,gjh->gih', tile_values, chosen)
    targets = jnp.arange(target_count, dtype=jnp.int32)
    selector = ((target_ids[None, :] == targets[:, None]) & is_live[None, :]).astype(jnp.float32)
    return jnp.einsum('rg,gih->rih', selector, products, precision=lax.Precision.HIGHEST)

def reference(features, adjacency, block_rows, block_cols, block_count, weight, bias_term, cotangent):
    feature_blocks = features.reshape(N_COL, CB, BS, H)
    cells = jnp.arange(N_ROW * N_COL, dtype=jnp.int32)

    def forward_cell(flat):
        row_id = flat // N_COL
        col_id = flat % N_COL
        is_live = jnp.arange(MAXBLK, dtype=jnp.int32) < block_count[row_id, col_id]
        part = block_sum(adjacency[row_id, col_id], feature_blocks[col_id], block_cols[row_id, col_id], block_rows[row_id, col_id], is_live, RB, False)
        return part.astype(jnp.bfloat16)
    partials = lax.map(forward_cell, cells).reshape(N_ROW, N_COL, SLAB_R, H)
    aggregate = lax.optimization_barrier(jnp.sum(partials.astype(jnp.float32), axis=1)).reshape(NODES, H).astype(jnp.bfloat16)
    pre_act = jnp.dot(aggregate, weight, preferred_element_type=jnp.float32) + bias_term.astype(jnp.float32)
    activated, pullback = jax.vjp(gelu_exact, pre_act)
    hidden_out = activated.astype(jnp.bfloat16)
    grad_pre = pullback(cotangent.astype(jnp.float32))[0].astype(jnp.bfloat16)
    factor = 1.0 / math.sqrt(NODES)
    grad_weight = lax.dot_general(aggregate, grad_pre, (((0,), (0,)), ((), ())), preferred_element_type=jnp.float32) * factor
    grad_bias = lax.optimization_barrier(jnp.sum(grad_pre.astype(jnp.float32), axis=0)) * factor
    grad_agg = jnp.dot(grad_pre, weight.T, preferred_element_type=jnp.float32).astype(jnp.bfloat16)
    grad_blocks = grad_agg.reshape(N_ROW, RB, BS, H)

    def backward_cell(flat):
        row_id = flat // N_COL
        col_id = flat % N_COL
        is_live = jnp.arange(MAXBLK, dtype=jnp.int32) < block_count[row_id, col_id]
        part = block_sum(adjacency[row_id, col_id], grad_blocks[row_id], block_rows[row_id, col_id], block_cols[row_id, col_id], is_live, CB, True)
        return part.astype(jnp.bfloat16)
    backs = lax.map(backward_cell, cells).reshape(N_ROW, N_COL, SLAB_C, H)
    grad_features = lax.optimization_barrier(jnp.sum(backs.astype(jnp.float32), axis=0)).reshape(NODES, H).astype(jnp.bfloat16)
    return (hidden_out, grad_weight, grad_bias, grad_features)
```

```python
import math

import jax
import jax.numpy as jnp
from jax import lax
from jax.experimental import pallas as pl
from jax.experimental.pallas import tpu as pltpu
from jax.sharding import PartitionSpec as P

H = 256
BS = 128
HALF = BS // 2
SLOTS = 32
TILE_ROWS = 16
TILE_COLS = 32
NODES = 65536
COPIES = 192
INV_SQRT2 = math.sqrt(0.5)
INV_SQRT_2PI = 1.0 / math.sqrt(2.0 * math.pi)


def f32(value):
    return value.astype(jnp.float32)


def chain_tables(keys, live, prev, last, targets):
    def prev_of(k, carry):
        key = keys[k]
        found = jnp.int32(0)
        for j in range(SLOTS - 1):
            hit = (keys[j] == key) & (j < k) & (j < live)
            found = jnp.where(hit, j + 1, found)
        prev[k] = found
        return carry

    lax.fori_loop(0, SLOTS, prev_of, 0)

    def last_of(t, carry):
        found = jnp.int32(0)
        for j in range(SLOTS):
            found = jnp.where((keys[j] == t) & (j < live), j + 1, found)
        last[t] = found
        return carry

    lax.fori_loop(0, targets, last_of, 0)


def kernel(
    features, adjacency, block_rows, block_cols, block_count, weight, bias_term, cotangent,
    hidden_out, weight_out, bias_out, features_out,
    tiles, slab, wgt, bias, cot, chain, part, gslab, back,
    prev_f, last_f, prev_b, last_b,
    y2p, y2m, ysp, ysm, yp_in, ym_in, mid,
    z2p, z2m, zsp, zsm, zp_in, zm_in,
    core_in, xsum, x2p, x2m, xsp, xsm, xp_in, xm_in, zout, zin,
    hid, fin, w0, w0_in, w1, w1_in, w2, w2_in, w3_in, w4_in, wfin, bfin,
    local_sem, send_sem, recv_sem,
):
    row = lax.axis_index("row")
    col = lax.axis_index("col")
    x, zl, core = row // 8, (row // 2) % 4, row % 2
    y, zh = col // 4, col % 4
    other = 1 - core
    xp, xm, x2 = (x + 1) % 4, (x + 3) % 4, (x + 2) % 4
    yp, ym, y2 = (y + 1) % 4, (y + 3) % 4, (y + 2) % 4
    zhp, zhm, zh2 = (zh + 1) % 4, (zh + 3) % 4, (zh + 2) % 4
    zl1, zl2, zl3 = zl + 1 - 2 * (zl % 2), (zl + 2) % 4, 3 - zl

    def at_row(x_=None, zl_=None, core_=None):
        x_ = x if x_ is None else x_
        zl_ = zl if zl_ is None else zl_
        core_ = core if core_ is None else core_
        return (x_ * 8 + zl_ * 2 + core_, col)

    def at_col(y_=None, zh_=None):
        y_ = y if y_ is None else y_
        zh_ = zh if zh_ is None else zh_
        return (row, y_ * 4 + zh_)

    def block_of(x_, zl_, core_):
        return x_ * 8 + zl_ * 2 + core_

    started = []

    def send(src, dst, to):
        i = len(started)
        copy = pltpu.make_async_remote_copy(
            src_ref=src, dst_ref=dst, send_sem=send_sem.at[i], recv_sem=recv_sem.at[i],
            device_id=to, device_id_type=pl.DeviceIdType.MESH,
        )
        copy.start()
        started.append(copy)
        return copy

    locals_started = []

    def local(src, dst):
        copy = pltpu.make_async_copy(src, dst, local_sem.at[len(locals_started)])
        copy.start()
        locals_started.append(copy)
        return copy

    own = block_of(x, zl, core)
    own_in = local(features, slab.at[own])
    tiles_in = local(adjacency, tiles)
    wgt_in = local(weight, wgt)
    bias_in = local(bias_term, bias)
    cot_in = local(cotangent, cot)

    peers = (
        [at_row(zl_=z) for z in (zl1, zl2, zl3)]
        + [at_row(x_=v) for v in (xp, xm, x2)]
        + [at_row(core_=other)]
        + [at_col(y_=v) for v in (yp, ym, y2)]
        + [at_col(zh_=v) for v in (zhp, zhm, zh2)]
    )
    barrier = pltpu.get_barrier_semaphore()
    for peer in peers:
        pl.semaphore_signal(barrier, inc=1, device_id=peer, device_id_type=pl.DeviceIdType.MESH)
    pl.semaphore_wait(barrier, len(peers))

    own_in.wait()
    z_in = [send(slab.at[own], slab.at[own], at_row(zl_=z)) for z in (zl1, zl2, zl3)]
    from_m, from_p, sib = [], [], []
    chunks = (zl, zl1, zl2, zl3)

    def relay(b):
        from_m.append(send(slab.at[b], slab.at[b], at_row(x_=xp)))
        from_p.append(send(slab.at[b], slab.at[b], at_row(x_=xm)))
        sib.append(send(slab.at[b], slab.at[b], at_row(core_=other)))

    relay(own)
    live = block_count[0]
    chain[0] = jnp.zeros((BS, H), jnp.float32)
    chain_tables(block_rows, live, prev_f, last_f, TILE_ROWS)
    for c in range(1, 4):
        z_in[c - 1].wait_recv()
        relay(block_of(x, chunks[c], core))
    lower, upper = pl.ds(0, HALF), pl.ds(HALF, HALF)
    far = []
    for c in range(4):
        from_m[c].wait_recv()
        b = block_of(xm, chunks[c], core)
        lo = send(slab.at[b, lower], slab.at[b, lower], at_row(x_=xp))
        sib.append(send(slab.at[b], slab.at[b], at_row(core_=other)))
        from_p[c].wait_recv()
        b = block_of(xp, chunks[c], core)
        hi = send(slab.at[b, upper], slab.at[b, upper], at_row(x_=xm))
        sib.append(send(slab.at[b], slab.at[b], at_row(core_=other)))
        far.append((lo, hi))
    for c in range(4):
        far[c][0].wait_recv()
        far[c][1].wait_recv()
        b = block_of(x2, chunks[c], core)
        sib.append(send(slab.at[b], slab.at[b], at_row(core_=other)))
    tiles_in.wait()
    for copy in sib:
        copy.wait_recv()

    def forward_slot(k, carry):
        product = jnp.dot(tiles[k], slab[block_cols[k]], preferred_element_type=jnp.float32)
        chain[k + 1] = product + chain[prev_f[k]]
        return carry

    lax.fori_loop(0, SLOTS, forward_slot, 0, unroll=4)

    def place(t):
        part[t] = chain[last_f[t]].astype(jnp.bfloat16)

    order = (zh2, zhp, zhm, zh)
    m2p, m2m, d1p, d1m, s1p, s1m = [], [], [], [], [], []
    for b in order:
        t = y2 * 4 + b
        place(t)
        m2p.append(send(part.at[t, lower], y2p.at[b], at_col(y_=yp)))
        m2m.append(send(part.at[t, upper], y2m.at[b], at_col(y_=ym)))
    for b in order:
        t = yp * 4 + b
        place(t)
        d1p.append(send(part.at[t, upper], yp_in.at[b, upper], at_col(y_=yp)))
        t = ym * 4 + b
        place(t)
        d1m.append(send(part.at[t, lower], ym_in.at[b, lower], at_col(y_=ym)))
    for b in order:
        place(y * 4 + b)
    for i, b in enumerate(order):
        m2p[i].wait_recv()
        ysp[b] = (f32(part[yp * 4 + b, lower]) + f32(y2p[b])).astype(jnp.bfloat16)
        s1p.append(send(ysp.at[b], yp_in.at[b, lower], at_col(y_=yp)))
        m2m[i].wait_recv()
        ysm[b] = (f32(part[ym * 4 + b, upper]) + f32(y2m[b])).astype(jnp.bfloat16)
        s1m.append(send(ysm.at[b], ym_in.at[b, upper], at_col(y_=ym)))

    def y_total(i):
        b = order[i]
        for copies in (d1p, d1m, s1p, s1m):
            copies[i].wait_recv()
        mid[b] = (f32(part[y * 4 + b]) + f32(yp_in[b]) + f32(ym_in[b])).astype(jnp.bfloat16)

    y_total(0)
    zm2p = send(mid.at[zh2, lower], z2p, at_col(zh_=zhp))
    zm2m = send(mid.at[zh2, upper], z2m, at_col(zh_=zhm))
    y_total(1)
    zd1p = send(mid.at[zhp, upper], zp_in.at[upper], at_col(zh_=zhp))
    y_total(2)
    zd1m = send(mid.at[zhm, lower], zm_in.at[lower], at_col(zh_=zhm))
    y_total(3)
    zm2p.wait_recv()
    zsp[...] = (f32(mid[zhp, lower]) + f32(z2p[...])).astype(jnp.bfloat16)
    zs1p = send(zsp, zp_in.at[lower], at_col(zh_=zhp))
    zm2m.wait_recv()
    zsm[...] = (f32(mid[zhm, upper]) + f32(z2m[...])).astype(jnp.bfloat16)
    zs1m = send(zsm, zm_in.at[upper], at_col(zh_=zhm))
    chain_tables(block_cols, live, prev_b, last_b, TILE_COLS)
    for copy in (wgt_in, bias_in, cot_in):
        copy.wait()
    for copy in (zd1p, zd1m, zs1p, zs1m):
        copy.wait_recv()
    agg = (f32(mid[zh]) + f32(zp_in[...]) + f32(zm_in[...])).astype(jnp.bfloat16)

    pre = jnp.dot(agg, wgt[...], preferred_element_type=jnp.float32) + bias[...]
    cdf = 0.5 * (1.0 + lax.erf(pre * INV_SQRT2))
    slope = cdf + pre * (jnp.exp(-0.5 * pre * pre) * INV_SQRT_2PI)
    grad_pre = (f32(cot[...]) * slope).astype(jnp.bfloat16)
    gslab[col] = lax.dot_general(
        grad_pre, wgt[...], (((1,), (1,)), ((), ())), preferred_element_type=jnp.float32
    ).astype(jnp.bfloat16)

    gz_m = send(gslab.at[col], gslab.at[col], at_col(zh_=zhp))
    gz_p = send(gslab.at[col], gslab.at[col], at_col(zh_=zhm))
    gy_m, gy_p = [], []

    def spread(b):
        gy_m.append(send(gslab.at[b], gslab.at[b], at_col(y_=yp)))
        gy_p.append(send(gslab.at[b], gslab.at[b], at_col(y_=ym)))

    spread(col)
    hid[...] = (pre * cdf).astype(jnp.bfloat16)
    hid_out = local(hid, hidden_out)
    grad_w = lax.dot_general(agg, grad_pre, (((0,), (0,)), ((), ())), preferred_element_type=jnp.float32)
    w0[0, 0:128] = grad_w[0:128]
    w0[1, 0:128] = grad_w[128:256]
    grad_b = jnp.broadcast_to(jnp.sum(f32(grad_pre), axis=0, keepdims=True), (8, H))
    w0[0, 128:136] = grad_b
    w0[1, 128:136] = grad_b
    wc = send(w0.at[other], w0_in, at_row(core_=other))

    gz_m.wait_recv()
    b = y * 4 + zhm
    gz2_lo = send(gslab.at[b, lower], gslab.at[b, lower], at_col(zh_=zhp))
    spread(b)
    gz_p.wait_recv()
    b = y * 4 + zhp
    gz2_hi = send(gslab.at[b, upper], gslab.at[b, upper], at_col(zh_=zhm))
    spread(b)

    wc.wait_recv()
    w_core = w0[core] + w0_in[...]
    for v in range(4):
        w1[v, 0:32] = w_core[32 * v : 32 * v + 32]
        w1[v, 32:40] = w_core[128:136]
    w1_in[x] = w1[x]
    wx = [send(w1.at[v], w1_in.at[x], at_row(x_=v)) for v in (xp, xm, x2)]

    g_far = []

    def spread_far(i):
        gy_m[i].wait_recv()
        b = ym * 4 + g_order[i]
        lo = send(gslab.at[b, lower], gslab.at[b, lower], at_col(y_=yp))
        gy_p[i].wait_recv()
        b = yp * 4 + g_order[i]
        hi = send(gslab.at[b, upper], gslab.at[b, upper], at_col(y_=ym))
        g_far.append((lo, hi))

    g_order = (zh, zhm, zhp, zh2)
    spread_far(0)
    gz2_lo.wait_recv()
    gz2_hi.wait_recv()
    spread(y * 4 + zh2)
    for i in range(1, 3):
        spread_far(i)
    for copy in wx:
        copy.wait_recv()
    w_x = w1_in[0] + w1_in[1] + w1_in[2] + w1_in[3]
    for v in range(4):
        w2[v, 0:8] = w_x[8 * v : 8 * v + 8]
        w2[v, 8:16] = w_x[32:40]
    w2_in[zl] = w2[zl]
    wz = [send(w2.at[v], w2_in.at[zl], at_row(zl_=v)) for v in (zl1, zl2, zl3)]
    spread_far(3)
    for pair in g_far:
        pair[0].wait_recv()
        pair[1].wait_recv()

    def backward_slot(k, carry):
        product = lax.dot_general(
            tiles[k], gslab[block_rows[k]], (((0,), (0,)), ((), ())), preferred_element_type=jnp.float32
        )
        chain[k + 1] = product + chain[prev_b[k]]
        return carry

    lax.fori_loop(0, SLOTS, backward_slot, 0, unroll=4)

    def place_back(t):
        back[t] = chain[last_b[t]].astype(jnp.bfloat16)

    zs = (zl, zl1, zl2, zl3)
    core_copies = {}
    for name, v in (("x2", x2), ("xp", xp), ("xm", xm), ("x", x)):
        for i, z in enumerate(zs):
            t = block_of(v, z, other)
            place_back(t)
            core_copies[name, i] = send(back.at[t], core_in.at[v * 4 + z], at_row(core_=other))
            place_back(block_of(v, z, core))

    for copy in wz:
        copy.wait_recv()
    w_z = w2_in[0] + w2_in[1] + w2_in[2] + w2_in[3]
    w3_in[y] = w_z
    wy = [send(w3_in.at[y], w3_in.at[y], at_col(y_=v)) for v in (yp, ym, y2)]

    def core_total(name, v, i):
        z = zs[i]
        core_copies[name, i].wait_recv()
        s = f32(back[block_of(v, z, core)]) + f32(core_in[v * 4 + z])
        xsum[v * 4 + z] = s.astype(jnp.bfloat16)

    m2p, m2m, d1p, d1m, s1p, s1m = [], [], [], [], [], []
    for i, z in enumerate(zs):
        core_total("x2", x2, i)
        m2p.append(send(xsum.at[x2 * 4 + z, lower], x2p.at[z], at_row(x_=xp)))
        m2m.append(send(xsum.at[x2 * 4 + z, upper], x2m.at[z], at_row(x_=xm)))
    for i, z in enumerate(zs):
        core_total("xp", xp, i)
        d1p.append(send(xsum.at[xp * 4 + z, upper], xp_in.at[z, upper], at_row(x_=xp)))
        core_total("xm", xm, i)
        d1m.append(send(xsum.at[xm * 4 + z, lower], xm_in.at[z, lower], at_row(x_=xm)))
    for i, z in enumerate(zs):
        core_total("x", x, i)

    for copy in wy:
        copy.wait_recv()
    w_y = w3_in[0] + w3_in[1] + w3_in[2] + w3_in[3]
    w4_in[zh] = w_y
    wh = [send(w4_in.at[zh], w4_in.at[zh], at_col(zh_=v)) for v in (zhp, zhm, zh2)]

    for i, z in enumerate(zs):
        m2p[i].wait_recv()
        xsp[z] = (f32(xsum[xp * 4 + z, lower]) + f32(x2p[z])).astype(jnp.bfloat16)
        s1p.append(send(xsp.at[z], xp_in.at[z, lower], at_row(x_=xp)))
        m2m[i].wait_recv()
        xsm[z] = (f32(xsum[xm * 4 + z, upper]) + f32(x2m[z])).astype(jnp.bfloat16)
        s1m.append(send(xsm.at[z], xm_in.at[z, upper], at_row(x_=xm)))

    for copy in wh:
        copy.wait_recv()
    factor = 1.0 / math.sqrt(NODES)
    w_all = (w4_in[0] + w4_in[1] + w4_in[2] + w4_in[3]) * factor
    bfin[...] = w_all[8:9]
    mine = core * 16 + x * 4 + zl
    wfin[mine] = w_all[0:8]
    b_out = local(bfin, bias_out)
    wgz = [send(wfin.at[mine], wfin.at[mine], at_row(zl_=v)) for v in (zl1, zl2, zl3)]

    z_final = []
    for i in (2, 3, 1, 0):
        z = zs[i]
        for copies in (d1p, d1m, s1p, s1m):
            copies[i].wait_recv()
        s = f32(xsum[x * 4 + z]) + f32(xp_in[z]) + f32(xm_in[z])
        zout[i] = s.astype(jnp.bfloat16)
        if i > 0:
            z_final.append(send(zout.at[i], zin.at[i], at_row(zl_=z)))

    for copy in wgz:
        copy.wait_recv()
    quarter = pl.ds(core * 16 + x * 4, 4)
    wgx = [send(wfin.at[quarter], wfin.at[quarter], at_row(x_=v)) for v in (xp, xm, x2)]
    for copy in z_final:
        copy.wait_recv()
    total = f32(zout[0]) + f32(zin[1]) + f32(zin[2]) + f32(zin[3])
    fin[...] = total.astype(jnp.bfloat16)
    fin_out = local(fin, features_out)
    for copy in wgx:
        copy.wait_recv()
    half = pl.ds(core * 16, 16)
    wgc = send(wfin.at[half], wfin.at[half], at_row(core_=other))
    wgc.wait_recv()
    w_out = local(wfin, weight_out)
    for copy in started:
        copy.wait_send()
    for copy in (hid_out, b_out, fin_out, w_out):
        copy.wait()


def shards(features, adjacency, block_rows, block_cols, block_count, weight, bias_term, cotangent):
    bf16, fp32 = jnp.bfloat16, jnp.float32
    vmem = pltpu.VMEM
    hbm = pl.BlockSpec(memory_space=pl.ANY)
    smem = pl.BlockSpec(memory_space=pltpu.SMEM)
    scratch = [
        vmem((SLOTS, BS, BS), bf16),
        vmem((TILE_COLS, BS, H), bf16),
        vmem((H, H), bf16),
        vmem((1, H), fp32),
        vmem((BS, H), bf16),
        vmem((SLOTS + 1, BS, H), fp32),
        vmem((TILE_ROWS, BS, H), bf16),
        vmem((TILE_ROWS, BS, H), bf16),
        vmem((TILE_COLS, BS, H), bf16),
        pltpu.SMEM((SLOTS,), jnp.int32),
        pltpu.SMEM((TILE_ROWS,), jnp.int32),
        pltpu.SMEM((SLOTS,), jnp.int32),
        pltpu.SMEM((TILE_COLS,), jnp.int32),
    ]
    scratch += [vmem((4, HALF, H), bf16)] * 4 + [vmem((4, BS, H), bf16)] * 3
    scratch += [vmem((HALF, H), bf16)] * 4 + [vmem((BS, H), bf16)] * 2
    scratch += [vmem((16, BS, H), bf16)] * 2
    scratch += [vmem((4, HALF, H), bf16)] * 4 + [vmem((4, BS, H), bf16)] * 4
    scratch += [vmem((BS, H), bf16)] * 2
    scratch += [
        vmem((2, 136, H), fp32),
        vmem((136, H), fp32),
        vmem((4, 40, H), fp32),
        vmem((4, 40, H), fp32),
        vmem((4, 16, H), fp32),
        vmem((4, 16, H), fp32),
        vmem((4, 16, H), fp32),
        vmem((4, 16, H), fp32),
        vmem((32, 8, H), fp32),
        vmem((1, H), fp32),
        pltpu.SemaphoreType.DMA((16,)),
        pltpu.SemaphoreType.DMA((COPIES,)),
        pltpu.SemaphoreType.DMA((COPIES,)),
    ]
    hidden, grad_weight, grad_bias, grad_features = pl.pallas_call(
        kernel,
        out_shape=(
            jax.ShapeDtypeStruct((BS, H), bf16),
            jax.ShapeDtypeStruct((32, 8, H), fp32),
            jax.ShapeDtypeStruct((1, H), fp32),
            jax.ShapeDtypeStruct((BS, H), bf16),
        ),
        in_specs=[hbm, hbm, smem, smem, smem, hbm, hbm, hbm],
        out_specs=(hbm, hbm, hbm, hbm),
        scratch_shapes=scratch,
        compiler_params=pltpu.CompilerParams(
            collective_id=0, has_side_effects=True, vmem_limit_bytes=48 * 1024 * 1024
        ),
        name="gcn_layer",
    )(
        features,
        adjacency.reshape(SLOTS, BS, BS),
        block_rows.reshape(SLOTS),
        block_cols.reshape(SLOTS),
        block_count.reshape(1),
        weight,
        bias_term.reshape(1, H),
        cotangent,
    )
    return hidden, grad_weight.reshape(H, H), grad_bias.reshape(H), grad_features


def solution(mesh):
    return jax.shard_map(
        shards,
        mesh=mesh,
        in_specs=(
            P(("col", "row"), None),
            P("row", "col", None, None, None),
            P("row", "col", None),
            P("row", "col", None),
            P("row", "col"),
            P(),
            P(),
            P(("row", "col"), None),
        ),
        out_specs=(P(("row", "col"), None), P(), P(), P(("col", "row"), None)),
        check_vma=False,
    )
```

```python
import math

import jax
import jax.numpy as jnp
from jax import lax
from jax.experimental import pallas as pl
from jax.experimental.pallas import tpu as pltpu
from jax.sharding import PartitionSpec as P

H = 256
BS = 128
COLS = 128
SLOTS = 32
TILE_ROWS = 16
TILE_COLS = 32
NODES = 65536
GROUP = 4
LOCALS = 14
SENDS = 16
RECVS = 66
INV_SQRT2 = math.sqrt(0.5)
INV_SQRT_2PI = 1.0 / math.sqrt(2.0 * math.pi)


def f32(value):
    return value.astype(jnp.float32)


def bf16(value):
    return value.astype(jnp.bfloat16)


def chain_tables(keys, live, prev, last, targets):
    def prev_of(k, carry):
        key = keys[k]
        found = jnp.int32(0)
        for j in range(SLOTS - 1):
            hit = (keys[j] == key) & (j < k) & (j < live)
            found = jnp.where(hit, j + 1, found)
        prev[k] = found
        return carry

    lax.fori_loop(0, SLOTS, prev_of, 0)

    def last_of(t, carry):
        found = jnp.int32(0)
        for j in range(SLOTS):
            found = jnp.where((keys[j] == t) & (j < live), j + 1, found)
        last[t] = found
        return carry

    lax.fori_loop(0, targets, last_of, 0)


def layer_kernel(
    features, adjacency, block_rows, block_cols, block_count, weight, bias_term, cotangent,
    hidden_out, weight_out, bias_out, features_out,
    tiles, wgt, bias, cot, chain, slab_a, slab_b, part, y_in, mid, zh_in, gslab_a, gslab_b, back, core_in, xsum, x_in, zl_out, zl_in,
    hid, fin, w0, w0_in, w1, w1_in, w2, w2_in, w3_in, w4_in, wfin, bfin,
    rows_s, cols_s, count_s, prev_f, last_f, prev_b, last_b,
    local_sem, send_sem, recv_sem,
):
    slab, gslab = (slab_a, slab_b), (gslab_a, gslab_b)
    row = lax.axis_index("row")
    col = lax.axis_index("col")
    x, zl, core = row // 8, (row // 2) % 4, row % 2
    y, zh = col // 4, col % 4
    other = 1 - core
    xs = ((x + 2) % 4, (x + 1) % 4, (x + 3) % 4)
    ys = ((y + 2) % 4, (y + 1) % 4, (y + 3) % 4)
    zhs = ((zh + 2) % 4, (zh + 1) % 4, (zh + 3) % 4)
    zls = ((zl + 2) % 4, 3 - zl, zl + 1 - 2 * (zl % 2))

    def block_of(x_, zl_, core_):
        return x_ * 8 + zl_ * 2 + core_

    def at_x(x_):
        return (block_of(x_, zl, core), col)

    def at_zl(zl_):
        return (block_of(x, zl_, core), col)

    def at_y(y_):
        return (row, y_ * 4 + zh)

    def at_zh(zh_):
        return (row, y * 4 + zh_)

    sibling = (block_of(x, zl, other), col)
    counts = {"send": 0, "recv": 0, "local": 0}

    def new(kind):
        counts[kind] += 1
        return counts[kind] - 1

    def send(src, dst, to, s, r):
        pltpu.make_async_remote_copy(
            src_ref=src, dst_ref=dst, send_sem=send_sem.at[s], recv_sem=recv_sem.at[r],
            device_id=to, device_id_type=pl.DeviceIdType.MESH,
        ).start()

    def whole(ref, s, r):
        return pltpu.make_async_remote_copy(
            src_ref=ref, dst_ref=ref, send_sem=send_sem.at[s], recv_sem=recv_sem.at[r],
            device_id=sibling, device_id_type=pl.DeviceIdType.MESH,
        )

    def arrived(r, ref):
        whole(ref, 0, r).wait_recv()

    def left(s, ref):
        whole(ref, s, 0).wait_send()

    def local(src, dst):
        copy = pltpu.make_async_copy(src, dst, local_sem.at[new("local")])
        copy.start()
        return copy

    def lanes(h):
        return pl.ds(COLS * h, COLS)

    own = block_of(x, zl, core)
    own_in = [local(features.at[:, lanes(h)], slab[h].at[own]) for h in range(2)]
    meta_in = [local(block_rows, rows_s), local(block_cols, cols_s), local(block_count, count_s)]
    tiles_in = local(adjacency, tiles)
    dense_in = [local(weight, wgt), local(bias_term, bias), local(cotangent, cot)]

    peers = [at_x(v) for v in xs] + [at_zl(v) for v in zls] + [sibling] + [at_y(v) for v in ys] + [at_zh(v) for v in zhs]
    barrier = pltpu.get_barrier_semaphore()
    for peer in peers:
        pl.semaphore_signal(barrier, inc=1, device_id=peer, device_id_type=pl.DeviceIdType.MESH)
    pl.semaphore_wait(barrier, len(peers))

    f_sent = [new("send") for _ in range(2)]
    fz = [[new("recv") for _ in range(3)] for _ in range(2)]
    fx = [[new("recv") for _ in range(4)] for _ in range(2)]
    fc = [new("recv") for _ in range(2)]
    f_zl = (zl,) + zls

    def to_core(h, b):
        send(slab[h].at[b], slab[h].at[b], sibling, f_sent[h], fc[h])

    def to_x(h, c):
        b = block_of(x, f_zl[c], core)
        for v in xs:
            send(slab[h].at[b], slab[h].at[b], at_x(v), f_sent[h], fx[h][c])
        to_core(h, b)

    for h in range(2):
        own_in[h].wait()
        for i in range(3):
            send(slab[h].at[own], slab[h].at[own], at_zl(zls[i]), f_sent[h], fz[h][i])
        to_x(h, 0)
    for copy in meta_in:
        copy.wait()
    live = count_s[0, 0]
    chain[0] = jnp.zeros((BS, COLS), jnp.float32)
    chain_tables(rows_s, live, prev_f, last_f, TILE_ROWS)
    near_first = (2, 0, 1)
    for h in range(2):
        for i in near_first:
            arrived(fz[h][i], slab[h].at[0])
            to_x(h, i + 1)

    def feature_half(h):
        for c in (0, 3, 1, 2):
            arrived(fx[h][c], slab[h].at[pl.ds(0, 3)])
            for v in xs:
                to_core(h, block_of(v, f_zl[c], core))
        arrived(fc[h], slab[h].at[pl.ds(0, 16)])

    def products(h, source, source_ids, prev, dims):
        def some(g, carry):
            terms = []
            for j in range(GROUP):
                k = g * GROUP + j
                terms.append(
                    lax.dot_general(
                        tiles[k], source[h][source_ids[k]], (dims, ((), ())), preferred_element_type=jnp.float32
                    )
                )
            for j in range(GROUP):
                k = g * GROUP + j
                chain[k + 1] = terms[j] + chain[prev[k]]
            return carry

        lax.fori_loop(0, SLOTS // GROUP, some, 0, unroll=2)

    p_sent = [new("send") for _ in range(2)]
    py = [[new("recv") for _ in range(4)] for _ in range(2)]
    pz = [new("recv") for _ in range(2)]
    p_zh = zhs + (zh,)

    def partial_half(h):
        products(h, slab, cols_s, prev_f, ((1,), (0,)))
        for i in range(4):
            for v in ys:
                t = v * 4 + p_zh[i]
                part[h, t] = bf16(chain[last_f[t]])
            for j in range(3):
                t = ys[j] * 4 + p_zh[i]
                send(part.at[h, t], y_in.at[h, i, j], at_y(ys[j]), p_sent[h], py[h][i])
        for i in range(4):
            t = y * 4 + p_zh[i]
            part[h, t] = bf16(chain[last_f[t]])

    def partial_total(h):
        for i in range(4):
            arrived(py[h][i], y_in.at[h, 0])
            s = f32(part[h, y * 4 + p_zh[i]]) + f32(y_in[h, i, 0]) + f32(y_in[h, i, 1]) + f32(y_in[h, i, 2])
            mid[h, i] = bf16(s)
            if i < 3:
                send(mid.at[h, i], zh_in.at[h, i], at_zh(p_zh[i]), p_sent[h], pz[h])

    feature_half(0)
    tiles_in.wait()
    partial_half(0)
    feature_half(1)
    partial_half(1)
    partial_total(0)
    partial_total(1)
    chain_tables(cols_s, live, prev_b, last_b, TILE_COLS)
    for copy in dense_in:
        copy.wait()
    agg = []
    for h in range(2):
        arrived(pz[h], zh_in.at[h])
        agg.append(bf16(f32(mid[h, 3]) + f32(zh_in[h, 0]) + f32(zh_in[h, 1]) + f32(zh_in[h, 2])))

    pre = bias[...] + jnp.dot(agg[0], wgt[0:COLS, :], preferred_element_type=jnp.float32)
    pre = pre + jnp.dot(agg[1], wgt[COLS:H, :], preferred_element_type=jnp.float32)
    cdf = 0.5 * (1.0 + lax.erf(pre * INV_SQRT2))
    slope = cdf + pre * (jnp.exp(-0.5 * pre * pre) * INV_SQRT_2PI)
    grad_pre = bf16(f32(cot[...]) * slope)
    grad_agg = bf16(
        lax.dot_general(grad_pre, wgt[...], (((1,), (1,)), ((), ())), preferred_element_type=jnp.float32)
    )

    g_sent = [new("send") for _ in range(2)]
    gz = [[new("recv") for _ in range(3)] for _ in range(2)]
    gy = [[new("recv") for _ in range(4)] for _ in range(2)]
    g_zh = (zh, zhs[0], zhs[2], zhs[1])

    def to_y(h, i):
        b = y * 4 + g_zh[i]
        for v in ys:
            send(gslab[h].at[b], gslab[h].at[b], at_y(v), g_sent[h], gy[h][i])

    for h in range(2):
        gslab[h][col] = grad_agg[:, COLS * h : COLS * h + COLS]
        for i in range(3):
            send(gslab[h].at[col], gslab[h].at[col], at_zh(zhs[i]), g_sent[h], gz[h][i])
        to_y(h, 0)
    hid[...] = bf16(pre * cdf)
    hid_out = local(hid, hidden_out)

    w_sent = [new("send") for _ in range(8)]
    w_recv = [new("recv") for _ in range(8)]
    both = jnp.concatenate(agg, axis=1)
    grad_w = lax.dot_general(both, grad_pre, (((0,), (0,)), ((), ())), preferred_element_type=jnp.float32)
    w0[0, 0:128] = grad_w[0:128]
    w0[1, 0:128] = grad_w[128:256]
    grad_b = jnp.broadcast_to(jnp.sum(f32(grad_pre), axis=0, keepdims=True), (8, H))
    w0[0, 128:136] = grad_b
    w0[1, 128:136] = grad_b
    send(w0.at[other], w0_in, sibling, w_sent[0], w_recv[0])

    def weight_x():
        arrived(w_recv[0], w0_in)
        s = w0[core] + w0_in[...]
        for v in range(4):
            w1[v, 0:32] = s[32 * v : 32 * v + 32]
            w1[v, 32:40] = s[128:136]
        w1_in[x] = w1[x]
        for v in xs:
            send(w1.at[v], w1_in.at[x], at_x(v), w_sent[1], w_recv[1])

    def weight_zl():
        arrived(w_recv[1], w1_in.at[pl.ds(0, 3)])
        s = w1_in[0] + w1_in[1] + w1_in[2] + w1_in[3]
        for v in range(4):
            w2[v, 0:8] = s[8 * v : 8 * v + 8]
            w2[v, 8:16] = s[32:40]
        w2_in[zl] = w2[zl]
        for v in zls:
            send(w2.at[v], w2_in.at[zl], at_zl(v), w_sent[2], w_recv[2])

    def weight_y():
        arrived(w_recv[2], w2_in.at[pl.ds(0, 3)])
        w3_in[y] = w2_in[0] + w2_in[1] + w2_in[2] + w2_in[3]
        for v in ys:
            send(w3_in.at[y], w3_in.at[y], at_y(v), w_sent[3], w_recv[3])

    def weight_zh():
        arrived(w_recv[3], w3_in.at[pl.ds(0, 3)])
        w4_in[zh] = w3_in[0] + w3_in[1] + w3_in[2] + w3_in[3]
        for v in zhs:
            send(w4_in.at[zh], w4_in.at[zh], at_zh(v), w_sent[4], w_recv[4])

    mine = core * 16 + x * 4 + zl

    def weight_back_zl():
        arrived(w_recv[4], w4_in.at[pl.ds(0, 3)])
        s = (w4_in[0] + w4_in[1] + w4_in[2] + w4_in[3]) * (1.0 / math.sqrt(NODES))
        bfin[...] = s[8:9]
        wfin[mine] = s[0:8]
        for v in zls:
            send(wfin.at[mine], wfin.at[mine], at_zl(v), w_sent[5], w_recv[5])
        return local(bfin, bias_out)

    def weight_back_x():
        arrived(w_recv[5], wfin.at[pl.ds(0, 3)])
        quarter = pl.ds(core * 16 + x * 4, 4)
        for v in xs:
            send(wfin.at[quarter], wfin.at[quarter], at_x(v), w_sent[6], w_recv[6])

    def weight_back_core():
        arrived(w_recv[6], wfin.at[pl.ds(0, 12)])
        half = pl.ds(core * 16, 16)
        send(wfin.at[half], wfin.at[half], sibling, w_sent[7], w_recv[7])

    weight_x()
    for i in range(3):
        arrived(gz[0][i], gslab[0].at[0])
        to_y(0, i + 1)
    weight_zl()
    for i in range(3):
        arrived(gz[1][i], gslab[1].at[0])
        to_y(1, i + 1)
    weight_y()

    b_sent = [new("send") for _ in range(2)]
    bc = [[new("recv") for _ in range(4)] for _ in range(2)]
    bx = [[new("recv") for _ in range(4)] for _ in range(2)]
    bz = [new("recv") for _ in range(2)]
    b_zl = zls + (zl,)

    def back_half(h):
        for i in range(4):
            arrived(gy[h][i], gslab[h].at[pl.ds(0, 3)])
        products(h, gslab, rows_s, prev_b, ((0,), (0,)))
        for i in range(4):
            for v in xs + (x,):
                t = block_of(v, b_zl[i], other)
                back[h, t] = bf16(chain[last_b[t]])
            for v in xs + (x,):
                t = block_of(v, b_zl[i], other)
                send(back.at[h, t], core_in.at[h, v * 4 + b_zl[i]], sibling, b_sent[h], bc[h][i])
        for i in range(4):
            for v in xs + (x,):
                t = block_of(v, b_zl[i], core)
                back[h, t] = bf16(chain[last_b[t]])

    def core_total(h):
        for i in range(4):
            arrived(bc[h][i], core_in.at[h, pl.ds(0, 4)])
            for v in xs + (x,):
                q = v * 4 + b_zl[i]
                xsum[h, q] = bf16(f32(back[h, block_of(v, b_zl[i], core)]) + f32(core_in[h, q]))
            for j in range(3):
                send(xsum.at[h, xs[j] * 4 + b_zl[i]], x_in.at[h, i, j], at_x(xs[j]), b_sent[h], bx[h][i])

    def x_total(h):
        for i in range(4):
            arrived(bx[h][i], x_in.at[h, 0])
            s = f32(xsum[h, x * 4 + b_zl[i]]) + f32(x_in[h, i, 0]) + f32(x_in[h, i, 1]) + f32(x_in[h, i, 2])
            zl_out[h, i] = bf16(s)
            if i < 3:
                send(zl_out.at[h, i], zl_in.at[h, i], at_zl(b_zl[i]), b_sent[h], bz[h])

    def z_total(h):
        arrived(bz[h], zl_in.at[h])
        s = f32(zl_out[h, 3]) + f32(zl_in[h, 0]) + f32(zl_in[h, 1]) + f32(zl_in[h, 2])
        fin[h] = bf16(s)
        return local(fin.at[h], features_out.at[:, lanes(h)])

    back_half(0)
    core_total(0)
    weight_zh()
    back_half(1)
    core_total(1)
    x_total(0)
    b_out = weight_back_zl()
    x_total(1)
    weight_back_x()
    outs = [z_total(0)]
    weight_back_core()
    outs.append(z_total(1))
    arrived(w_recv[7], wfin.at[pl.ds(0, 16)])
    outs += [local(wfin, weight_out), hid_out, b_out]
    for h in range(2):
        left(f_sent[h], slab[h].at[pl.ds(0, 31)])
        left(p_sent[h], part.at[h, pl.ds(0, 15)])
        left(g_sent[h], gslab[h].at[pl.ds(0, 15)])
        left(b_sent[h], back.at[h, pl.ds(0, 31)])
    left(w_sent[0], w0_in)
    left(w_sent[1], w1_in.at[pl.ds(0, 3)])
    for i in (2, 3, 4):
        left(w_sent[i], w2_in.at[pl.ds(0, 3)])
    left(w_sent[5], wfin.at[pl.ds(0, 3)])
    left(w_sent[6], wfin.at[pl.ds(0, 12)])
    left(w_sent[7], wfin.at[pl.ds(0, 16)])
    for copy in outs:
        copy.wait()
    assert counts == {"send": SENDS, "recv": RECVS, "local": LOCALS}, counts


def write_kernel(hidden, weight, bias, features, hidden_out, weight_out, bias_out, features_out, h, w, b, f, sems):
    trios = ((features, f, features_out), (weight, w, weight_out), (hidden, h, hidden_out), (bias, b, bias_out))
    reads = [pltpu.make_async_copy(src, held, sems.at[i]) for i, (src, held, _) in enumerate(trios)]
    writes = [pltpu.make_async_copy(held, dst, sems.at[4 + i]) for i, (_, held, dst) in enumerate(trios)]
    for copy in reads:
        copy.start()
    for read, write in zip(reads, writes):
        read.wait()
        write.start()
    for copy in writes:
        copy.wait()


def shards(features, adjacency, block_rows, block_cols, block_count, weight, bias_term, cotangent):
    half, single = jnp.bfloat16, jnp.float32
    vmem = pltpu.VMEM
    hbm = pl.BlockSpec(memory_space=pl.ANY)
    scratch = [
        vmem((SLOTS, BS, BS), half),
        vmem((H, H), half),
        vmem((1, H), single),
        vmem((BS, H), half),
        vmem((SLOTS + 1, BS, COLS), single),
        vmem((TILE_COLS, BS, COLS), half),
        vmem((TILE_COLS, BS, COLS), half),
        vmem((2, TILE_ROWS, BS, COLS), half),
        vmem((2, 4, 3, BS, COLS), half),
        vmem((2, 4, BS, COLS), half),
        vmem((2, 3, BS, COLS), half),
        vmem((TILE_ROWS, BS, COLS), half),
        vmem((TILE_ROWS, BS, COLS), half),
        vmem((2, TILE_COLS, BS, COLS), half),
        vmem((2, 16, BS, COLS), half),
        vmem((2, 16, BS, COLS), half),
        vmem((2, 4, 3, BS, COLS), half),
        vmem((2, 4, BS, COLS), half),
        vmem((2, 3, BS, COLS), half),
        vmem((BS, H), half),
        vmem((2, BS, COLS), half),
        vmem((2, 136, H), single),
        vmem((136, H), single),
        vmem((4, 40, H), single),
        vmem((4, 40, H), single),
        vmem((4, 16, H), single),
        vmem((4, 16, H), single),
        vmem((4, 16, H), single),
        vmem((4, 16, H), single),
        vmem((32, 8, H), single),
        vmem((1, H), single),
        pltpu.SMEM((SLOTS,), jnp.int32),
        pltpu.SMEM((SLOTS,), jnp.int32),
        pltpu.SMEM((1, 1), jnp.int32),
        pltpu.SMEM((SLOTS,), jnp.int32),
        pltpu.SMEM((TILE_ROWS,), jnp.int32),
        pltpu.SMEM((SLOTS,), jnp.int32),
        pltpu.SMEM((TILE_COLS,), jnp.int32),
        pltpu.SemaphoreType.DMA((LOCALS,)),
        pltpu.SemaphoreType.DMA((SENDS,)),
        pltpu.SemaphoreType.DMA((RECVS,)),
    ]
    shapes = (
        jax.ShapeDtypeStruct((BS, H), half),
        jax.ShapeDtypeStruct((32, 8, H), single),
        jax.ShapeDtypeStruct((1, H), single),
        jax.ShapeDtypeStruct((BS, H), half),
    )
    results = pl.pallas_call(
        layer_kernel,
        out_shape=shapes,
        in_specs=[hbm] * 8,
        out_specs=(hbm,) * 4,
        scratch_shapes=scratch,
        compiler_params=pltpu.CompilerParams(
            collective_id=0, has_side_effects=True, vmem_limit_bytes=60 * 1024 * 1024
        ),
        name="gcn_layer",
    )(
        features,
        adjacency.reshape(SLOTS, BS, BS),
        block_rows.reshape(SLOTS),
        block_cols.reshape(SLOTS),
        block_count,
        weight,
        bias_term.reshape(1, H),
        cotangent,
    )
    hidden, grad_weight, grad_bias, grad_features = pl.pallas_call(
        write_kernel,
        out_shape=shapes,
        in_specs=[hbm] * 4,
        out_specs=(hbm,) * 4,
        scratch_shapes=[vmem(v.shape, v.dtype) for v in shapes] + [pltpu.SemaphoreType.DMA((8,))],
        compiler_params=pltpu.CompilerParams(vmem_limit_bytes=60 * 1024 * 1024),
        name="write_results",
    )(*results)
    return hidden, grad_weight.reshape(H, H), grad_bias.reshape(H), grad_features


def solution(mesh):
    return jax.shard_map(
        shards,
        mesh=mesh,
        in_specs=(
            P(("col", "row"), None),
            P("row", "col", None, None, None),
            P("row", "col", None),
            P("row", "col", None),
            P("row", "col"),
            P(),
            P(),
            P(("row", "col"), None),
        ),
        out_specs=(P(("row", "col"), None), P(), P(), P(("col", "row"), None)),
        check_vma=False,
    )
```

```python
import math

import jax
import jax.numpy as jnp
from jax import lax
from jax.experimental import pallas as pl
from jax.experimental.pallas import tpu as pltpu
from jax.sharding import PartitionSpec as P

H = 256
BS = 128
COLS = 128
SLOTS = 32
TILE_ROWS = 16
TILE_COLS = 32
NODES = 65536
GROUP = 4
LOCALS = 14
SENDS = 16
RECVS = 66
INV_SQRT2 = math.sqrt(0.5)
INV_SQRT_2PI = 1.0 / math.sqrt(2.0 * math.pi)


def f32(value):
    return value.astype(jnp.float32)


def bf16(value):
    return value.astype(jnp.bfloat16)


def chain_tables(keys, live, prev, last, targets):
    def prev_of(k, carry):
        key = keys[k]
        found = jnp.int32(0)
        for j in range(SLOTS - 1):
            hit = (keys[j] == key) & (j < k) & (j < live)
            found = jnp.where(hit, j + 1, found)
        prev[k] = found
        return carry

    lax.fori_loop(0, SLOTS, prev_of, 0)

    def last_of(t, carry):
        found = jnp.int32(0)
        for j in range(SLOTS):
            found = jnp.where((keys[j] == t) & (j < live), j + 1, found)
        last[t] = found
        return carry

    lax.fori_loop(0, targets, last_of, 0)


def layer_kernel(
    features, adjacency, block_rows, block_cols, block_count, weight, bias_term, cotangent,
    hidden_out, weight_out, bias_out, features_out,
    tiles, wgt, bias, cot, chain, slab_a, slab_b, part, y_in, mid, zh_in, gslab_a, gslab_b, back, core_in, xsum, x_in, zl_out, zl_in,
    hid, fin, w0, w0_in, w1, w1_in, w2_in, w3, w3_in, w4_in, wfin, bfin,
    rows_s, cols_s, count_s, prev_f, last_f, prev_b, last_b,
    local_sem, send_sem, recv_sem,
):
    slab, gslab = (slab_a, slab_b), (gslab_a, gslab_b)
    row = lax.axis_index("row")
    col = lax.axis_index("col")
    x, zl, core = row // 8, (row // 2) % 4, row % 2
    y, zh = col // 4, col % 4
    other = 1 - core
    xs = ((x + 2) % 4, (x + 1) % 4, (x + 3) % 4)
    ys = ((y + 2) % 4, (y + 1) % 4, (y + 3) % 4)
    zhs = ((zh + 2) % 4, (zh + 1) % 4, (zh + 3) % 4)
    zls = ((zl + 2) % 4, 3 - zl, zl + 1 - 2 * (zl % 2))

    def block_of(x_, zl_, core_):
        return x_ * 8 + zl_ * 2 + core_

    def at_x(x_):
        return (block_of(x_, zl, core), col)

    def at_zl(zl_):
        return (block_of(x, zl_, core), col)

    def at_y(y_):
        return (row, y_ * 4 + zh)

    def at_zh(zh_):
        return (row, y * 4 + zh_)

    sibling = (block_of(x, zl, other), col)
    counts = {"send": 0, "recv": 0, "local": 0}

    def new(kind):
        counts[kind] += 1
        return counts[kind] - 1

    def send(src, dst, to, s, r):
        pltpu.make_async_remote_copy(
            src_ref=src, dst_ref=dst, send_sem=send_sem.at[s], recv_sem=recv_sem.at[r],
            device_id=to, device_id_type=pl.DeviceIdType.MESH,
        ).start()

    def whole(ref, s, r):
        return pltpu.make_async_remote_copy(
            src_ref=ref, dst_ref=ref, send_sem=send_sem.at[s], recv_sem=recv_sem.at[r],
            device_id=sibling, device_id_type=pl.DeviceIdType.MESH,
        )

    def arrived(r, ref):
        whole(ref, 0, r).wait_recv()

    def left(s, ref):
        whole(ref, s, 0).wait_send()

    def local(src, dst):
        copy = pltpu.make_async_copy(src, dst, local_sem.at[new("local")])
        copy.start()
        return copy

    def lanes(h):
        return pl.ds(COLS * h, COLS)

    own = block_of(x, zl, core)
    own_in = [local(features.at[:, lanes(h)], slab[h].at[own]) for h in range(2)]
    meta_in = [local(block_rows, rows_s), local(block_cols, cols_s), local(block_count, count_s)]
    tiles_in = local(adjacency, tiles)
    dense_in = [local(weight, wgt), local(bias_term, bias), local(cotangent, cot)]

    peers = [at_zh(v) for v in zhs] + [at_zl(v) for v in zls] + [at_x(v) for v in xs] + [at_y(v) for v in ys] + [sibling]
    barrier = pltpu.get_barrier_semaphore()
    for peer in peers:
        pl.semaphore_signal(barrier, inc=1, device_id=peer, device_id_type=pl.DeviceIdType.MESH)
    pl.semaphore_wait(barrier, len(peers))

    f_sent = [new("send") for _ in range(2)]
    fz = [[new("recv") for _ in range(3)] for _ in range(2)]
    fx = [[new("recv") for _ in range(4)] for _ in range(2)]
    fc = [new("recv") for _ in range(2)]
    f_zl = (zl,) + zls

    def to_core(h, b):
        send(slab[h].at[b], slab[h].at[b], sibling, f_sent[h], fc[h])

    def to_x(h, c):
        b = block_of(x, f_zl[c], core)
        for v in xs:
            send(slab[h].at[b], slab[h].at[b], at_x(v), f_sent[h], fx[h][c])
        to_core(h, b)

    def to_zl(h):
        for i in range(3):
            send(slab[h].at[own], slab[h].at[own], at_zl(zls[i]), f_sent[h], fz[h][i])

    own_in[0].wait()
    to_zl(0)
    to_x(0, 0)
    own_in[1].wait()
    to_x(1, 0)
    for copy in meta_in:
        copy.wait()
    live = count_s[0, 0]
    chain[0] = jnp.zeros((BS, COLS), jnp.float32)
    near_first = (2, 0, 1)
    for h in range(2):
        for i in near_first:
            arrived(fz[h][i], slab[h].at[0])
            to_x(h, i + 1)
            if (h, i) == (0, 2):
                to_zl(1)
    chain_tables(rows_s, live, prev_f, last_f, TILE_ROWS)

    def feature_half(h):
        for c in (0, 3, 1, 2):
            arrived(fx[h][c], slab[h].at[pl.ds(0, 3)])
            for v in xs:
                to_core(h, block_of(v, f_zl[c], core))
        arrived(fc[h], slab[h].at[pl.ds(0, 16)])

    def products(h, source, source_ids, prev, dims):
        def some(g, carry):
            terms = []
            for j in range(GROUP):
                k = g * GROUP + j
                terms.append(
                    lax.dot_general(
                        tiles[k], source[h][source_ids[k]], (dims, ((), ())), preferred_element_type=jnp.float32
                    )
                )
            for j in range(GROUP):
                k = g * GROUP + j
                chain[k + 1] = terms[j] + chain[prev[k]]
            return carry

        lax.fori_loop(0, SLOTS // GROUP, some, 0, unroll=2)

    class Ring:
        def __init__(self, h, to, at, source, sent, into):
            self.h, self.to, self.at, self.source, self.sent, self.into = h, to, at, source, sent, into
            self.sem = [new("recv") for _ in range(4)]

        def terms(self, i):
            for j in range(3):
                v = self.to[j]
                send(self.source(v, i), self.into.at[self.h, i, j], self.at(v), self.sent, self.sem[i])

        def total(self, i, own_term):
            arrived(self.sem[i], self.into.at[self.h, i])
            s = f32(own_term)
            for j in range(3):
                s = s + f32(self.into[self.h, i, j])
            return bf16(s)

    p_sent = [new("send") for _ in range(2)]
    p_zh = zhs + (zh,)
    p_ring = [
        Ring(h, ys, at_y, lambda v, i, h=h: part.at[h, v * 4 + p_zh[i]], p_sent[h], y_in)
        for h in range(2)
    ]
    pz = [new("recv") for _ in range(2)]

    def partial_place(h, i):
        for v in ys + (y,):
            t = v * 4 + p_zh[i]
            part[h, t] = bf16(chain[last_f[t]])

    def partial_total(h):
        for i in range(4):
            mid[h, i] = p_ring[h].total(i, part[h, y * 4 + p_zh[i]])
            if i < 3:
                send(mid.at[h, i], zh_in.at[h, i], at_zh(p_zh[i]), p_sent[h], pz[h])

    feature_half(0)
    tiles_in.wait()
    products(0, slab, cols_s, prev_f, ((1,), (0,)))
    for i in range(4):
        partial_place(0, i)
        p_ring[0].terms(i)
    feature_half(1)
    products(1, slab, cols_s, prev_f, ((1,), (0,)))
    for i in range(4):
        partial_place(1, i)
        p_ring[1].terms(i)
    partial_total(0)
    partial_total(1)
    chain_tables(cols_s, live, prev_b, last_b, TILE_COLS)
    for copy in dense_in:
        copy.wait()
    agg = []
    for h in range(2):
        arrived(pz[h], zh_in.at[h])
        agg.append(bf16(f32(mid[h, 3]) + f32(zh_in[h, 0]) + f32(zh_in[h, 1]) + f32(zh_in[h, 2])))

    pre = bias[...] + jnp.dot(agg[0], wgt[0:COLS, :], preferred_element_type=jnp.float32)
    pre = pre + jnp.dot(agg[1], wgt[COLS:H, :], preferred_element_type=jnp.float32)
    cdf = 0.5 * (1.0 + lax.erf(pre * INV_SQRT2))
    slope = cdf + pre * (jnp.exp(-0.5 * pre * pre) * INV_SQRT_2PI)
    grad_pre = bf16(f32(cot[...]) * slope)
    grad_agg = bf16(
        lax.dot_general(grad_pre, wgt[...], (((1,), (1,)), ((), ())), preferred_element_type=jnp.float32)
    )

    g_sent = [new("send") for _ in range(2)]
    gz = [[new("recv") for _ in range(3)] for _ in range(2)]
    gy = [[new("recv") for _ in range(4)] for _ in range(2)]
    g_zh = (zh, zhs[0], zhs[2], zhs[1])

    def to_y(h, i):
        b = y * 4 + g_zh[i]
        for v in ys:
            send(gslab[h].at[b], gslab[h].at[b], at_y(v), g_sent[h], gy[h][i])

    def to_zh(h, i):
        send(gslab[h].at[col], gslab[h].at[col], at_zh(zhs[i]), g_sent[h], gz[h][i])

    for h in range(2):
        gslab[h][col] = grad_agg[:, COLS * h : COLS * h + COLS]
        if h == 0:
            for i in (1, 2, 0):
                to_zh(0, i)
        to_y(h, 0)
    hid[...] = bf16(pre * cdf)
    hid_out = local(hid, hidden_out)

    w_sent = [new("send") for _ in range(8)]
    w_recv = [new("recv") for _ in range(8)]
    both = jnp.concatenate(agg, axis=1)
    grad_w = lax.dot_general(both, grad_pre, (((0,), (0,)), ((), ())), preferred_element_type=jnp.float32)
    w0[0, 0:128] = grad_w[0:128]
    w0[1, 0:128] = grad_w[128:256]
    grad_b = jnp.broadcast_to(jnp.sum(f32(grad_pre), axis=0, keepdims=True), (8, H))
    w0[0, 128:136] = grad_b
    w0[1, 128:136] = grad_b
    send(w0.at[other], w0_in, sibling, w_sent[0], w_recv[0])

    def weight_x():
        arrived(w_recv[0], w0_in)
        s = w0[core] + w0_in[...]
        for v in range(4):
            w1[v, 0:32] = s[32 * v : 32 * v + 32]
            w1[v, 32:40] = s[128:136]
        w1_in[x] = w1[x]
        for v in xs:
            send(w1.at[v], w1_in.at[x], at_x(v), w_sent[1], w_recv[1])

    def weight_y():
        arrived(w_recv[1], w1_in.at[pl.ds(0, 3)])
        w2_in[y] = w1_in[0] + w1_in[1] + w1_in[2] + w1_in[3]
        for v in ys:
            send(w2_in.at[y], w2_in.at[y], at_y(v), w_sent[2], w_recv[2])

    def weight_zl():
        arrived(w_recv[2], w2_in.at[pl.ds(0, 3)])
        s = w2_in[0] + w2_in[1] + w2_in[2] + w2_in[3]
        for v in range(4):
            w3[v, 0:8] = s[8 * v : 8 * v + 8]
            w3[v, 8:16] = s[32:40]
        w3_in[zl] = w3[zl]
        for v in zls:
            send(w3.at[v], w3_in.at[zl], at_zl(v), w_sent[3], w_recv[3])

    def weight_zh():
        arrived(w_recv[3], w3_in.at[pl.ds(0, 3)])
        w4_in[zh] = w3_in[0] + w3_in[1] + w3_in[2] + w3_in[3]
        for v in zhs:
            send(w4_in.at[zh], w4_in.at[zh], at_zh(v), w_sent[4], w_recv[4])

    mine = core * 16 + x * 4 + zl

    def weight_back_zl():
        arrived(w_recv[4], w4_in.at[pl.ds(0, 3)])
        s = (w4_in[0] + w4_in[1] + w4_in[2] + w4_in[3]) * (1.0 / math.sqrt(NODES))
        bfin[...] = s[8:9]
        wfin[mine] = s[0:8]
        for v in zls:
            send(wfin.at[mine], wfin.at[mine], at_zl(v), w_sent[5], w_recv[5])
        return local(bfin, bias_out)

    def weight_back_x():
        arrived(w_recv[5], wfin.at[pl.ds(0, 3)])
        quarter = pl.ds(core * 16 + x * 4, 4)
        for v in xs:
            send(wfin.at[quarter], wfin.at[quarter], at_x(v), w_sent[6], w_recv[6])

    def weight_back_core():
        arrived(w_recv[6], wfin.at[pl.ds(0, 12)])
        half = pl.ds(core * 16, 16)
        send(wfin.at[half], wfin.at[half], sibling, w_sent[7], w_recv[7])

    def gradient_relay(h, i):
        arrived(gz[h][i], gslab[h].at[0])
        to_y(h, i + 1)

    weight_x()
    weight_y()
    for i in (1, 2, 0):
        to_zh(1, i)
    for i in (1, 2, 0):
        gradient_relay(0, i)
    weight_zl()
    for i in (1, 2, 0):
        gradient_relay(1, i)
    weight_zh()

    b_sent = [new("send") for _ in range(2)]
    bc = [[new("recv") for _ in range(4)] for _ in range(2)]
    bz = [new("recv") for _ in range(2)]
    b_zl = zls + (zl,)
    b_ring = [
        Ring(h, xs, at_x, lambda v, i, h=h: xsum.at[h, v * 4 + b_zl[i]], b_sent[h], x_in)
        for h in range(2)
    ]

    def back_half(h):
        for i in range(4):
            arrived(gy[h][i], gslab[h].at[pl.ds(0, 3)])
        products(h, gslab, rows_s, prev_b, ((0,), (0,)))
        for i in range(4):
            for v in xs + (x,):
                t = block_of(v, b_zl[i], other)
                back[h, t] = bf16(chain[last_b[t]])
            for v in xs + (x,):
                t = block_of(v, b_zl[i], other)
                send(back.at[h, t], core_in.at[h, v * 4 + b_zl[i]], sibling, b_sent[h], bc[h][i])
        for i in range(4):
            for v in xs + (x,):
                t = block_of(v, b_zl[i], core)
                back[h, t] = bf16(chain[last_b[t]])

    def core_total(h, i):
        arrived(bc[h][i], core_in.at[h, pl.ds(0, 4)])
        for v in xs + (x,):
            q = v * 4 + b_zl[i]
            xsum[h, q] = bf16(f32(back[h, block_of(v, b_zl[i], core)]) + f32(core_in[h, q]))

    def x_total(h, i):
        zl_out[h, i] = b_ring[h].total(i, xsum[h, x * 4 + b_zl[i]])
        if i < 3:
            send(zl_out.at[h, i], zl_in.at[h, i], at_zl(b_zl[i]), b_sent[h], bz[h])

    def z_total(h):
        arrived(bz[h], zl_in.at[h])
        s = f32(zl_out[h, 3]) + f32(zl_in[h, 0]) + f32(zl_in[h, 1]) + f32(zl_in[h, 2])
        fin[h] = bf16(s)
        return local(fin.at[h], features_out.at[:, lanes(h)])

    back_half(0)
    for i in range(4):
        core_total(0, i)
        b_ring[0].terms(i)
    back_half(1)
    for i in range(4):
        core_total(1, i)
        b_ring[1].terms(i)
    for i in range(4):
        x_total(0, i)
    b_out = weight_back_zl()
    x_total(1, 0)
    x_total(1, 1)
    weight_back_x()
    x_total(1, 2)
    x_total(1, 3)
    outs = [z_total(0)]
    weight_back_core()
    outs.append(z_total(1))
    arrived(w_recv[7], wfin.at[pl.ds(0, 16)])
    outs += [local(wfin, weight_out), hid_out, b_out]
    for h in range(2):
        left(f_sent[h], slab[h].at[pl.ds(0, 31)])
        left(p_sent[h], part.at[h, pl.ds(0, 15)])
        left(g_sent[h], gslab[h].at[pl.ds(0, 15)])
        left(b_sent[h], back.at[h, pl.ds(0, 31)])
    left(w_sent[0], w0_in)
    left(w_sent[1], w1_in.at[pl.ds(0, 3)])
    left(w_sent[2], w2_in.at[pl.ds(0, 3)])
    left(w_sent[3], w3_in.at[pl.ds(0, 3)])
    left(w_sent[4], w4_in.at[pl.ds(0, 3)])
    left(w_sent[5], wfin.at[pl.ds(0, 3)])
    left(w_sent[6], wfin.at[pl.ds(0, 12)])
    left(w_sent[7], wfin.at[pl.ds(0, 16)])
    for copy in outs:
        copy.wait()
    assert counts == {"send": SENDS, "recv": RECVS, "local": LOCALS}, counts


def write_kernel(hidden, weight, bias, features, hidden_out, weight_out, bias_out, features_out, h, w, b, f, sems):
    trios = ((features, f, features_out), (weight, w, weight_out), (hidden, h, hidden_out), (bias, b, bias_out))
    reads = [pltpu.make_async_copy(src, held, sems.at[i]) for i, (src, held, _) in enumerate(trios)]
    writes = [pltpu.make_async_copy(held, dst, sems.at[4 + i]) for i, (_, held, dst) in enumerate(trios)]
    for copy in reads:
        copy.start()
    for read, write in zip(reads, writes):
        read.wait()
        write.start()
    for copy in writes:
        copy.wait()


def shards(features, adjacency, block_rows, block_cols, block_count, weight, bias_term, cotangent):
    half, single = jnp.bfloat16, jnp.float32
    vmem = pltpu.VMEM
    hbm = pl.BlockSpec(memory_space=pl.ANY)
    scratch = [
        vmem((SLOTS, BS, BS), half),
        vmem((H, H), half),
        vmem((1, H), single),
        vmem((BS, H), half),
        vmem((SLOTS + 1, BS, COLS), single),
        vmem((TILE_COLS, BS, COLS), half),
        vmem((TILE_COLS, BS, COLS), half),
        vmem((2, TILE_ROWS, BS, COLS), half),
        vmem((2, 4, 3, BS, COLS), half),
        vmem((2, 4, BS, COLS), half),
        vmem((2, 3, BS, COLS), half),
        vmem((TILE_ROWS, BS, COLS), half),
        vmem((TILE_ROWS, BS, COLS), half),
        vmem((2, TILE_COLS, BS, COLS), half),
        vmem((2, 16, BS, COLS), half),
        vmem((2, 16, BS, COLS), half),
        vmem((2, 4, 3, BS, COLS), half),
        vmem((2, 4, BS, COLS), half),
        vmem((2, 3, BS, COLS), half),
        vmem((BS, H), half),
        vmem((2, BS, COLS), half),
        vmem((2, 136, H), single),
        vmem((136, H), single),
        vmem((4, 40, H), single),
        vmem((4, 40, H), single),
        vmem((4, 40, H), single),
        vmem((4, 16, H), single),
        vmem((4, 16, H), single),
        vmem((4, 16, H), single),
        vmem((32, 8, H), single),
        vmem((1, H), single),
        pltpu.SMEM((SLOTS,), jnp.int32),
        pltpu.SMEM((SLOTS,), jnp.int32),
        pltpu.SMEM((1, 1), jnp.int32),
        pltpu.SMEM((SLOTS,), jnp.int32),
        pltpu.SMEM((TILE_ROWS,), jnp.int32),
        pltpu.SMEM((SLOTS,), jnp.int32),
        pltpu.SMEM((TILE_COLS,), jnp.int32),
        pltpu.SemaphoreType.DMA((LOCALS,)),
        pltpu.SemaphoreType.DMA((SENDS,)),
        pltpu.SemaphoreType.DMA((RECVS,)),
    ]
    shapes = (
        jax.ShapeDtypeStruct((BS, H), half),
        jax.ShapeDtypeStruct((32, 8, H), single),
        jax.ShapeDtypeStruct((1, H), single),
        jax.ShapeDtypeStruct((BS, H), half),
    )
    results = pl.pallas_call(
        layer_kernel,
        out_shape=shapes,
        in_specs=[hbm] * 8,
        out_specs=(hbm,) * 4,
        scratch_shapes=scratch,
        compiler_params=pltpu.CompilerParams(
            collective_id=0, has_side_effects=True, vmem_limit_bytes=60 * 1024 * 1024
        ),
        name="gcn_layer",
    )(
        features,
        adjacency.reshape(SLOTS, BS, BS),
        block_rows.reshape(SLOTS),
        block_cols.reshape(SLOTS),
        block_count,
        weight,
        bias_term.reshape(1, H),
        cotangent,
    )
    hidden, grad_weight, grad_bias, grad_features = pl.pallas_call(
        write_kernel,
        out_shape=shapes,
        in_specs=[hbm] * 4,
        out_specs=(hbm,) * 4,
        scratch_shapes=[vmem(v.shape, v.dtype) for v in shapes] + [pltpu.SemaphoreType.DMA((8,))],
        compiler_params=pltpu.CompilerParams(vmem_limit_bytes=60 * 1024 * 1024),
        name="write_results",
    )(*results)
    return hidden, grad_weight.reshape(H, H), grad_bias.reshape(H), grad_features


def solution(mesh):
    return jax.shard_map(
        shards,
        mesh=mesh,
        in_specs=(
            P(("col", "row"), None),
            P("row", "col", None, None, None),
            P("row", "col", None),
            P("row", "col", None),
            P("row", "col"),
            P(),
            P(),
            P(("row", "col"), None),
        ),
        out_specs=(P(("row", "col"), None), P(), P(), P(("col", "row"), None)),
        check_vma=False,
    )
```

```python
import math

import jax
import jax.numpy as jnp
from jax import lax
from jax.experimental import pallas as pl
from jax.experimental.pallas import tpu as pltpu
from jax.sharding import PartitionSpec as P

H = 256
BS = 128
COLS = 128
SLOTS = 32
TILE_ROWS = 16
TILE_COLS = 32
NODES = 65536
GROUP = 4
LOCALS = 14
SENDS = 16
RECVS = 66
INV_SQRT2 = math.sqrt(0.5)
INV_SQRT_2PI = 1.0 / math.sqrt(2.0 * math.pi)


def f32(value):
    return value.astype(jnp.float32)


def bf16(value):
    return value.astype(jnp.bfloat16)


def chain_tables(keys, live, prev, last, targets):
    def prev_of(k, carry):
        key = keys[k]
        found = jnp.int32(0)
        for j in range(SLOTS - 1):
            hit = (keys[j] == key) & (j < k) & (j < live)
            found = jnp.where(hit, j + 1, found)
        prev[k] = found
        return carry

    lax.fori_loop(0, SLOTS, prev_of, 0)

    def last_of(t, carry):
        found = jnp.int32(0)
        for j in range(SLOTS):
            found = jnp.where((keys[j] == t) & (j < live), j + 1, found)
        last[t] = found
        return carry

    lax.fori_loop(0, targets, last_of, 0)


def layer_kernel(
    features, adjacency, block_rows, block_cols, block_count, weight, bias_term, cotangent,
    hidden_out, weight_out, bias_out, features_out,
    tiles, wgt, bias, cot, chain, slab_a, slab_b, part, y_in, mid, zh_in, gslab_a, gslab_b, back, core_in, xsum, x_in, zl_out, zl_in,
    hid, fin, w0, w0_in, w1, w1_in, w2_in, w3, w3_in, w4_in, wfin, bfin,
    rows_s, cols_s, count_s, prev_f, last_f, prev_b, last_b,
    local_sem, send_sem, recv_sem,
):
    slab, gslab = (slab_a, slab_b), (gslab_a, gslab_b)
    row = lax.axis_index("row")
    col = lax.axis_index("col")
    x, zl, core = row // 8, (row // 2) % 4, row % 2
    y, zh = col // 4, col % 4
    other = 1 - core
    xs = ((x + 2) % 4, (x + 1) % 4, (x + 3) % 4)
    ys = ((y + 2) % 4, (y + 1) % 4, (y + 3) % 4)
    zhs = ((zh + 2) % 4, (zh + 1) % 4, (zh + 3) % 4)
    zls = ((zl + 2) % 4, 3 - zl, zl + 1 - 2 * (zl % 2))

    def block_of(x_, zl_, core_):
        return x_ * 8 + zl_ * 2 + core_

    def at_x(x_):
        return (block_of(x_, zl, core), col)

    def at_zl(zl_):
        return (block_of(x, zl_, core), col)

    def at_y(y_):
        return (row, y_ * 4 + zh)

    def at_zh(zh_):
        return (row, y * 4 + zh_)

    sibling = (block_of(x, zl, other), col)
    counts = {"send": 0, "recv": 0, "local": 0}

    def new(kind):
        counts[kind] += 1
        return counts[kind] - 1

    def send(src, dst, to, s, r):
        pltpu.make_async_remote_copy(
            src_ref=src, dst_ref=dst, send_sem=send_sem.at[s], recv_sem=recv_sem.at[r],
            device_id=to, device_id_type=pl.DeviceIdType.MESH,
        ).start()

    def whole(ref, s, r):
        return pltpu.make_async_remote_copy(
            src_ref=ref, dst_ref=ref, send_sem=send_sem.at[s], recv_sem=recv_sem.at[r],
            device_id=sibling, device_id_type=pl.DeviceIdType.MESH,
        )

    def arrived(r, ref):
        whole(ref, 0, r).wait_recv()

    def left(s, ref):
        whole(ref, s, 0).wait_send()

    def local(src, dst):
        copy = pltpu.make_async_copy(src, dst, local_sem.at[new("local")])
        copy.start()
        return copy

    def lanes(h):
        return pl.ds(COLS * h, COLS)

    own = block_of(x, zl, core)
    own_in = [local(features.at[:, lanes(h)], slab[h].at[own]) for h in range(2)]
    meta_in = [local(block_rows, rows_s), local(block_cols, cols_s), local(block_count, count_s)]
    tiles_in = local(adjacency, tiles)
    dense_in = [local(weight, wgt), local(bias_term, bias), local(cotangent, cot)]

    peers = [at_zh(v) for v in zhs] + [at_zl(v) for v in zls] + [at_x(v) for v in xs] + [at_y(v) for v in ys] + [sibling]
    barrier = pltpu.get_barrier_semaphore()
    for peer in peers:
        pl.semaphore_signal(barrier, inc=1, device_id=peer, device_id_type=pl.DeviceIdType.MESH)
    pl.semaphore_wait(barrier, len(peers))

    f_sent = [new("send") for _ in range(2)]
    fz = [[new("recv") for _ in range(3)] for _ in range(2)]
    fx = [[new("recv") for _ in range(4)] for _ in range(2)]
    fc = [new("recv") for _ in range(2)]
    f_zl = (zl,) + zls

    def to_core(h, b):
        send(slab[h].at[b], slab[h].at[b], sibling, f_sent[h], fc[h])

    def to_x(h, c):
        b = block_of(x, f_zl[c], core)
        for v in xs:
            send(slab[h].at[b], slab[h].at[b], at_x(v), f_sent[h], fx[h][c])
        to_core(h, b)

    def to_zl(h):
        for i in range(3):
            send(slab[h].at[own], slab[h].at[own], at_zl(zls[i]), f_sent[h], fz[h][i])

    own_in[0].wait()
    to_zl(0)
    to_x(0, 0)
    own_in[1].wait()
    to_x(1, 0)
    for copy in meta_in:
        copy.wait()
    live = count_s[0, 0]
    chain[0] = jnp.zeros((BS, COLS), jnp.float32)
    near_first = (2, 0, 1)
    for h in range(2):
        for i in near_first:
            arrived(fz[h][i], slab[h].at[0])
            to_x(h, i + 1)
            if (h, i) == (0, 2):
                to_zl(1)
    chain_tables(rows_s, live, prev_f, last_f, TILE_ROWS)

    def feature_half(h):
        for c in (0, 3, 1, 2):
            arrived(fx[h][c], slab[h].at[pl.ds(0, 3)])
            for v in xs:
                to_core(h, block_of(v, f_zl[c], core))
        arrived(fc[h], slab[h].at[pl.ds(0, 16)])

    def products(h, source, source_ids, prev, dims):
        def some(g, carry):
            terms = []
            for j in range(GROUP):
                k = g * GROUP + j
                terms.append(
                    lax.dot_general(
                        tiles[k], source[h][source_ids[k]], (dims, ((), ())), preferred_element_type=jnp.float32
                    )
                )
            for j in range(GROUP):
                k = g * GROUP + j
                chain[k + 1] = terms[j] + chain[prev[k]]
            return carry

        lax.fori_loop(0, SLOTS // GROUP, some, 0, unroll=2)

    class Ring:
        def __init__(self, h, to, at, source, sent, into):
            self.h, self.to, self.at, self.source, self.sent, self.into = h, to, at, source, sent, into
            self.sem = [new("recv") for _ in range(4)]

        def terms(self, i):
            for j in range(3):
                v = self.to[j]
                send(self.source(v, i), self.into.at[self.h, i, j], self.at(v), self.sent, self.sem[i])

        def total(self, i, own_term):
            arrived(self.sem[i], self.into.at[self.h, i])
            s = f32(own_term)
            for j in range(3):
                s = s + f32(self.into[self.h, i, j])
            return bf16(s)

    p_sent = [new("send") for _ in range(2)]
    p_zh = zhs + (zh,)
    p_ring = [
        Ring(h, ys, at_y, lambda v, i, h=h: part.at[h, v * 4 + p_zh[i]], p_sent[h], y_in)
        for h in range(2)
    ]
    pz = [new("recv") for _ in range(2)]

    def partial_place(h, i):
        for v in ys + (y,):
            t = v * 4 + p_zh[i]
            part[h, t] = bf16(chain[last_f[t]])

    def partial_total(h):
        for i in range(4):
            mid[h, i] = p_ring[h].total(i, part[h, y * 4 + p_zh[i]])
            if i < 3:
                send(mid.at[h, i], zh_in.at[h, i], at_zh(p_zh[i]), p_sent[h], pz[h])

    feature_half(0)
    tiles_in.wait()
    products(0, slab, cols_s, prev_f, ((1,), (0,)))
    for i in range(4):
        partial_place(0, i)
        p_ring[0].terms(i)
    feature_half(1)
    products(1, slab, cols_s, prev_f, ((1,), (0,)))
    for i in range(4):
        partial_place(1, i)
        p_ring[1].terms(i)
    partial_total(0)
    partial_total(1)
    chain_tables(cols_s, live, prev_b, last_b, TILE_COLS)
    for copy in dense_in:
        copy.wait()
    agg = []
    for h in range(2):
        arrived(pz[h], zh_in.at[h])
        agg.append(bf16(f32(mid[h, 3]) + f32(zh_in[h, 0]) + f32(zh_in[h, 1]) + f32(zh_in[h, 2])))

    pre = bias[...] + jnp.dot(agg[0], wgt[0:COLS, :], preferred_element_type=jnp.float32)
    pre = pre + jnp.dot(agg[1], wgt[COLS:H, :], preferred_element_type=jnp.float32)
    cdf = 0.5 * (1.0 + lax.erf(pre * INV_SQRT2))
    slope = cdf + pre * (jnp.exp(-0.5 * pre * pre) * INV_SQRT_2PI)
    grad_pre = bf16(f32(cot[...]) * slope)
    grad_agg = bf16(
        lax.dot_general(grad_pre, wgt[...], (((1,), (1,)), ((), ())), preferred_element_type=jnp.float32)
    )

    g_sent = [new("send") for _ in range(2)]
    gz = [[new("recv") for _ in range(3)] for _ in range(2)]
    gy = [[new("recv") for _ in range(4)] for _ in range(2)]
    g_zh = (zh, zhs[0], zhs[2], zhs[1])

    def to_y(h, i):
        b = y * 4 + g_zh[i]
        for v in ys:
            send(gslab[h].at[b], gslab[h].at[b], at_y(v), g_sent[h], gy[h][i])

    def to_zh(h, i):
        send(gslab[h].at[col], gslab[h].at[col], at_zh(zhs[i]), g_sent[h], gz[h][i])

    for h in range(2):
        gslab[h][col] = grad_agg[:, COLS * h : COLS * h + COLS]
        if h == 0:
            for i in (1, 2, 0):
                to_zh(0, i)
        to_y(h, 0)
    hid[...] = bf16(pre * cdf)
    hid_out = local(hid, hidden_out)

    w_sent = [new("send") for _ in range(8)]
    w_recv = [new("recv") for _ in range(8)]
    both = jnp.concatenate(agg, axis=1)
    grad_w = lax.dot_general(both, grad_pre, (((0,), (0,)), ((), ())), preferred_element_type=jnp.float32)
    w0[0, 0:128] = grad_w[0:128]
    w0[1, 0:128] = grad_w[128:256]
    grad_b = jnp.broadcast_to(jnp.sum(f32(grad_pre), axis=0, keepdims=True), (8, H))
    w0[0, 128:136] = grad_b
    w0[1, 128:136] = grad_b
    send(w0.at[other], w0_in, sibling, w_sent[0], w_recv[0])

    def weight_x():
        arrived(w_recv[0], w0_in)
        s = w0[core] + w0_in[...]
        for v in range(4):
            w1[v, 0:32] = s[32 * v : 32 * v + 32]
            w1[v, 32:40] = s[128:136]
        w1_in[x] = w1[x]
        for v in xs:
            send(w1.at[v], w1_in.at[x], at_x(v), w_sent[1], w_recv[1])

    def weight_y():
        arrived(w_recv[1], w1_in.at[pl.ds(0, 3)])
        w2_in[y] = w1_in[0] + w1_in[1] + w1_in[2] + w1_in[3]
        for v in ys:
            send(w2_in.at[y], w2_in.at[y], at_y(v), w_sent[2], w_recv[2])

    def weight_zl():
        arrived(w_recv[2], w2_in.at[pl.ds(0, 3)])
        s = w2_in[0] + w2_in[1] + w2_in[2] + w2_in[3]
        for v in range(4):
            w3[v, 0:8] = s[8 * v : 8 * v + 8]
            w3[v, 8:16] = s[32:40]
        w3_in[zl] = w3[zl]
        for v in zls:
            send(w3.at[v], w3_in.at[zl], at_zl(v), w_sent[3], w_recv[3])

    def weight_zh():
        arrived(w_recv[3], w3_in.at[pl.ds(0, 3)])
        w4_in[zh] = w3_in[0] + w3_in[1] + w3_in[2] + w3_in[3]
        for v in zhs:
            send(w4_in.at[zh], w4_in.at[zh], at_zh(v), w_sent[4], w_recv[4])

    mine = core * 16 + x * 4 + zl

    def weight_back_zl():
        arrived(w_recv[4], w4_in.at[pl.ds(0, 3)])
        s = (w4_in[0] + w4_in[1] + w4_in[2] + w4_in[3]) * (1.0 / math.sqrt(NODES))
        bfin[...] = s[8:9]
        wfin[mine] = s[0:8]
        for v in zls:
            send(wfin.at[mine], wfin.at[mine], at_zl(v), w_sent[5], w_recv[5])
        return local(bfin, bias_out)

    def weight_back_x():
        arrived(w_recv[5], wfin.at[pl.ds(0, 3)])
        quarter = pl.ds(core * 16 + x * 4, 4)
        for v in xs:
            send(wfin.at[quarter], wfin.at[quarter], at_x(v), w_sent[6], w_recv[6])

    def weight_back_core():
        arrived(w_recv[6], wfin.at[pl.ds(0, 12)])
        half = pl.ds(core * 16, 16)
        send(wfin.at[half], wfin.at[half], sibling, w_sent[7], w_recv[7])

    def gradient_relay(h, i):
        arrived(gz[h][i], gslab[h].at[0])
        to_y(h, i + 1)

    b_sent = [new("send") for _ in range(2)]
    bc = [[new("recv") for _ in range(4)] for _ in range(2)]
    bz = [new("recv") for _ in range(2)]
    b_zl = zls + (zl,)
    b_ring = [
        Ring(h, xs, at_x, lambda v, i, h=h: xsum.at[h, v * 4 + b_zl[i]], b_sent[h], x_in)
        for h in range(2)
    ]

    def back_half(h):
        for i in range(4):
            arrived(gy[h][i], gslab[h].at[pl.ds(0, 3)])
        products(h, gslab, rows_s, prev_b, ((0,), (0,)))
        for i in range(4):
            for v in xs + (x,):
                t = block_of(v, b_zl[i], other)
                back[h, t] = bf16(chain[last_b[t]])
            for v in xs + (x,):
                t = block_of(v, b_zl[i], other)
                send(back.at[h, t], core_in.at[h, v * 4 + b_zl[i]], sibling, b_sent[h], bc[h][i])
        for i in range(4):
            for v in xs + (x,):
                t = block_of(v, b_zl[i], core)
                back[h, t] = bf16(chain[last_b[t]])

    def core_total(h, i):
        arrived(bc[h][i], core_in.at[h, pl.ds(0, 4)])
        for v in xs + (x,):
            q = v * 4 + b_zl[i]
            xsum[h, q] = bf16(f32(back[h, block_of(v, b_zl[i], core)]) + f32(core_in[h, q]))

    def x_total(h, i):
        zl_out[h, i] = b_ring[h].total(i, xsum[h, x * 4 + b_zl[i]])
        if i < 3:
            send(zl_out.at[h, i], zl_in.at[h, i], at_zl(b_zl[i]), b_sent[h], bz[h])

    def z_total(h):
        arrived(bz[h], zl_in.at[h])
        s = f32(zl_out[h, 3]) + f32(zl_in[h, 0]) + f32(zl_in[h, 1]) + f32(zl_in[h, 2])
        fin[h] = bf16(s)
        return local(fin.at[h], features_out.at[:, lanes(h)])

    def core_half(h):
        for i in range(4):
            core_total(h, i)
            b_ring[h].terms(i)

    weight_x()
    weight_y()
    for i in (1, 2, 0):
        to_zh(1, i)
    for i in (1, 2, 0):
        gradient_relay(0, i)
    weight_zl()
    gradient_relay(1, 1)
    gradient_relay(1, 2)
    weight_zh()
    back_half(0)
    gradient_relay(1, 0)
    core_half(0)
    back_half(1)
    core_half(1)
    b_out = weight_back_zl()
    for i in range(4):
        x_total(0, i)
    weight_back_x()
    for i in range(4):
        x_total(1, i)
    outs = [z_total(0)]
    weight_back_core()
    outs.append(z_total(1))
    arrived(w_recv[7], wfin.at[pl.ds(0, 16)])
    outs += [local(wfin, weight_out), hid_out, b_out]
    for h in range(2):
        left(f_sent[h], slab[h].at[pl.ds(0, 31)])
        left(p_sent[h], part.at[h, pl.ds(0, 15)])
        left(g_sent[h], gslab[h].at[pl.ds(0, 15)])
        left(b_sent[h], back.at[h, pl.ds(0, 31)])
    left(w_sent[0], w0_in)
    left(w_sent[1], w1_in.at[pl.ds(0, 3)])
    left(w_sent[2], w2_in.at[pl.ds(0, 3)])
    left(w_sent[3], w3_in.at[pl.ds(0, 3)])
    left(w_sent[4], w4_in.at[pl.ds(0, 3)])
    left(w_sent[5], wfin.at[pl.ds(0, 3)])
    left(w_sent[6], wfin.at[pl.ds(0, 12)])
    left(w_sent[7], wfin.at[pl.ds(0, 16)])
    for copy in outs:
        copy.wait()
    assert counts == {"send": SENDS, "recv": RECVS, "local": LOCALS}, counts


def write_kernel(hidden, weight, bias, features, hidden_out, weight_out, bias_out, features_out, h, w, b, f, sems):
    trios = ((features, f, features_out), (weight, w, weight_out), (hidden, h, hidden_out), (bias, b, bias_out))
    reads = [pltpu.make_async_copy(src, held, sems.at[i]) for i, (src, held, _) in enumerate(trios)]
    writes = [pltpu.make_async_copy(held, dst, sems.at[4 + i]) for i, (_, held, dst) in enumerate(trios)]
    for copy in reads:
        copy.start()
    for read, write in zip(reads, writes):
        read.wait()
        write.start()
    for copy in writes:
        copy.wait()


def shards(features, adjacency, block_rows, block_cols, block_count, weight, bias_term, cotangent):
    half, single = jnp.bfloat16, jnp.float32
    vmem = pltpu.VMEM
    hbm = pl.BlockSpec(memory_space=pl.ANY)
    scratch = [
        vmem((SLOTS, BS, BS), half),
        vmem((H, H), half),
        vmem((1, H), single),
        vmem((BS, H), half),
        vmem((SLOTS + 1, BS, COLS), single),
        vmem((TILE_COLS, BS, COLS), half),
        vmem((TILE_COLS, BS, COLS), half),
        vmem((2, TILE_ROWS, BS, COLS), half),
        vmem((2, 4, 3, BS, COLS), half),
        vmem((2, 4, BS, COLS), half),
        vmem((2, 3, BS, COLS), half),
        vmem((TILE_ROWS, BS, COLS), half),
        vmem((TILE_ROWS, BS, COLS), half),
        vmem((2, TILE_COLS, BS, COLS), half),
        vmem((2, 16, BS, COLS), half),
        vmem((2, 16, BS, COLS), half),
        vmem((2, 4, 3, BS, COLS), half),
        vmem((2, 4, BS, COLS), half),
        vmem((2, 3, BS, COLS), half),
        vmem((BS, H), half),
        vmem((2, BS, COLS), half),
        vmem((2, 136, H), single),
        vmem((136, H), single),
        vmem((4, 40, H), single),
        vmem((4, 40, H), single),
        vmem((4, 40, H), single),
        vmem((4, 16, H), single),
        vmem((4, 16, H), single),
        vmem((4, 16, H), single),
        vmem((32, 8, H), single),
        vmem((1, H), single),
        pltpu.SMEM((SLOTS,), jnp.int32),
        pltpu.SMEM((SLOTS,), jnp.int32),
        pltpu.SMEM((1, 1), jnp.int32),
        pltpu.SMEM((SLOTS,), jnp.int32),
        pltpu.SMEM((TILE_ROWS,), jnp.int32),
        pltpu.SMEM((SLOTS,), jnp.int32),
        pltpu.SMEM((TILE_COLS,), jnp.int32),
        pltpu.SemaphoreType.DMA((LOCALS,)),
        pltpu.SemaphoreType.DMA((SENDS,)),
        pltpu.SemaphoreType.DMA((RECVS,)),
    ]
    shapes = (
        jax.ShapeDtypeStruct((BS, H), half),
        jax.ShapeDtypeStruct((32, 8, H), single),
        jax.ShapeDtypeStruct((1, H), single),
        jax.ShapeDtypeStruct((BS, H), half),
    )
    results = pl.pallas_call(
        layer_kernel,
        out_shape=shapes,
        in_specs=[hbm] * 8,
        out_specs=(hbm,) * 4,
        scratch_shapes=scratch,
        compiler_params=pltpu.CompilerParams(
            collective_id=0, has_side_effects=True, vmem_limit_bytes=60 * 1024 * 1024
        ),
        name="gcn_layer",
    )(
        features,
        adjacency.reshape(SLOTS, BS, BS),
        block_rows.reshape(SLOTS),
        block_cols.reshape(SLOTS),
        block_count,
        weight,
        bias_term.reshape(1, H),
        cotangent,
    )
    hidden, grad_weight, grad_bias, grad_features = pl.pallas_call(
        write_kernel,
        out_shape=shapes,
        in_specs=[hbm] * 4,
        out_specs=(hbm,) * 4,
        scratch_shapes=[vmem(v.shape, v.dtype) for v in shapes] + [pltpu.SemaphoreType.DMA((8,))],
        compiler_params=pltpu.CompilerParams(vmem_limit_bytes=60 * 1024 * 1024),
        name="write_results",
    )(*results)
    return hidden, grad_weight.reshape(H, H), grad_bias.reshape(H), grad_features


def solution(mesh):
    return jax.shard_map(
        shards,
        mesh=mesh,
        in_specs=(
            P(("col", "row"), None),
            P("row", "col", None, None, None),
            P("row", "col", None),
            P("row", "col", None),
            P("row", "col"),
            P(),
            P(),
            P(("row", "col"), None),
        ),
        out_specs=(P(("row", "col"), None), P(), P(), P(("col", "row"), None)),
        check_vma=False,
    )
```

```python
import math

import jax
import jax.numpy as jnp
from jax import lax
from jax.experimental import pallas as pl
from jax.experimental.pallas import tpu as pltpu
from jax.sharding import PartitionSpec as P

H = 256
BS = 128
COLS = 128
SLOTS = 32
TILE_ROWS = 16
TILE_COLS = 32
NODES = 65536
GROUP = 4
LOCALS = 14
SENDS = 16
RECVS = 66
INV_SQRT2 = math.sqrt(0.5)
INV_SQRT_2PI = 1.0 / math.sqrt(2.0 * math.pi)


def f32(value):
    return value.astype(jnp.float32)


def bf16(value):
    return value.astype(jnp.bfloat16)


def chain_tables(keys, live, prev, last, targets):
    def prev_of(k, carry):
        key = keys[k]
        found = jnp.int32(0)
        for j in range(SLOTS - 1):
            hit = (keys[j] == key) & (j < k) & (j < live)
            found = jnp.where(hit, j + 1, found)
        prev[k] = found
        return carry

    lax.fori_loop(0, SLOTS, prev_of, 0)

    def last_of(t, carry):
        found = jnp.int32(0)
        for j in range(SLOTS):
            found = jnp.where((keys[j] == t) & (j < live), j + 1, found)
        last[t] = found
        return carry

    lax.fori_loop(0, targets, last_of, 0)


def layer_kernel(
    features, adjacency, block_rows, block_cols, block_count, weight, bias_term, cotangent,
    hidden_out, weight_out, bias_out, features_out,
    tiles, turned, wgt, bias, cot, chain, slab_a, slab_b, part, y_in, mid, zh_in, gslab_a, gslab_b, back, core_in, xsum, x_in, zl_out, zl_in,
    hid, fin, w0, w0_in, w1, w1_in, w2_in, w3, w3_in, w4_in, wfin, bfin,
    rows_s, cols_s, count_s, prev_f, last_f, prev_b, last_b,
    local_sem, send_sem, recv_sem,
):
    slab, gslab = (slab_a, slab_b), (gslab_a, gslab_b)
    row = lax.axis_index("row")
    col = lax.axis_index("col")
    x, zl, core = row // 8, (row // 2) % 4, row % 2
    y, zh = col // 4, col % 4
    other = 1 - core
    xs = ((x + 2) % 4, (x + 1) % 4, (x + 3) % 4)
    ys = ((y + 2) % 4, (y + 1) % 4, (y + 3) % 4)
    zhs = ((zh + 2) % 4, (zh + 1) % 4, (zh + 3) % 4)
    zls = ((zl + 2) % 4, 3 - zl, zl + 1 - 2 * (zl % 2))

    def block_of(x_, zl_, core_):
        return x_ * 8 + zl_ * 2 + core_

    def at_x(x_):
        return (block_of(x_, zl, core), col)

    def at_zl(zl_):
        return (block_of(x, zl_, core), col)

    def at_y(y_):
        return (row, y_ * 4 + zh)

    def at_zh(zh_):
        return (row, y * 4 + zh_)

    sibling = (block_of(x, zl, other), col)
    counts = {"send": 0, "recv": 0, "local": 0}

    def new(kind):
        counts[kind] += 1
        return counts[kind] - 1

    def send(src, dst, to, s, r):
        pltpu.make_async_remote_copy(
            src_ref=src, dst_ref=dst, send_sem=send_sem.at[s], recv_sem=recv_sem.at[r],
            device_id=to, device_id_type=pl.DeviceIdType.MESH,
        ).start()

    def whole(ref, s, r):
        return pltpu.make_async_remote_copy(
            src_ref=ref, dst_ref=ref, send_sem=send_sem.at[s], recv_sem=recv_sem.at[r],
            device_id=sibling, device_id_type=pl.DeviceIdType.MESH,
        )

    def arrived(r, ref):
        whole(ref, 0, r).wait_recv()

    def left(s, ref):
        whole(ref, s, 0).wait_send()

    def local(src, dst):
        copy = pltpu.make_async_copy(src, dst, local_sem.at[new("local")])
        copy.start()
        return copy

    def lanes(h):
        return pl.ds(COLS * h, COLS)

    own = block_of(x, zl, core)
    own_in = [local(features.at[:, lanes(h)], slab[h].at[own]) for h in range(2)]
    meta_in = [local(block_rows, rows_s), local(block_cols, cols_s), local(block_count, count_s)]
    tiles_in = local(adjacency, tiles)
    dense_in = [local(weight, wgt), local(bias_term, bias), local(cotangent, cot)]

    peers = [at_zh(v) for v in zhs] + [at_zl(v) for v in zls] + [at_x(v) for v in xs] + [at_y(v) for v in ys] + [sibling]
    barrier = pltpu.get_barrier_semaphore()
    for peer in peers:
        pl.semaphore_signal(barrier, inc=1, device_id=peer, device_id_type=pl.DeviceIdType.MESH)
    pl.semaphore_wait(barrier, len(peers))

    f_sent = [new("send") for _ in range(2)]
    fz = [[new("recv") for _ in range(3)] for _ in range(2)]
    fx = [[new("recv") for _ in range(4)] for _ in range(2)]
    fc = [new("recv") for _ in range(2)]
    f_zl = (zl,) + zls

    def to_core(h, b):
        send(slab[h].at[b], slab[h].at[b], sibling, f_sent[h], fc[h])

    def to_x(h, c):
        b = block_of(x, f_zl[c], core)
        for v in xs:
            send(slab[h].at[b], slab[h].at[b], at_x(v), f_sent[h], fx[h][c])
        to_core(h, b)

    def to_zl(h):
        for i in range(3):
            send(slab[h].at[own], slab[h].at[own], at_zl(zls[i]), f_sent[h], fz[h][i])

    own_in[0].wait()
    to_zl(0)
    to_x(0, 0)
    own_in[1].wait()
    to_x(1, 0)
    for copy in meta_in:
        copy.wait()
    live = count_s[0, 0]
    chain[0] = jnp.zeros((BS, COLS), jnp.float32)
    near_first = (2, 0, 1)
    for h in range(2):
        for i in near_first:
            arrived(fz[h][i], slab[h].at[0])
            to_x(h, i + 1)
            if (h, i) == (0, 2):
                to_zl(1)
    chain_tables(rows_s, live, prev_f, last_f, TILE_ROWS)

    def feature_half(h):
        for c in (0, 3, 1, 2):
            arrived(fx[h][c], slab[h].at[pl.ds(0, 3)])
            for v in xs:
                to_core(h, block_of(v, f_zl[c], core))
        arrived(fc[h], slab[h].at[pl.ds(0, 16)])

    def products(h, table, source, source_ids, prev):
        def some(g, carry):
            terms = []
            for j in range(GROUP):
                k = g * GROUP + j
                terms.append(
                    jnp.dot(table[k], source[h][source_ids[k]], preferred_element_type=jnp.float32)
                )
            for j in range(GROUP):
                k = g * GROUP + j
                chain[k + 1] = terms[j] + chain[prev[k]]
            return carry

        lax.fori_loop(0, SLOTS // GROUP, some, 0, unroll=4)

    class Ring:
        def __init__(self, h, to, at, source, sent, into):
            self.h, self.to, self.at, self.source, self.sent, self.into = h, to, at, source, sent, into
            self.sem = [new("recv") for _ in range(4)]

        def terms(self, i):
            for j in range(3):
                v = self.to[j]
                send(self.source(v, i), self.into.at[self.h, i, j], self.at(v), self.sent, self.sem[i])

        def total(self, i, own_term):
            arrived(self.sem[i], self.into.at[self.h, i])
            s = f32(own_term)
            for j in range(3):
                s = s + f32(self.into[self.h, i, j])
            return bf16(s)

    p_sent = [new("send") for _ in range(2)]
    p_zh = zhs + (zh,)
    p_ring = [
        Ring(h, ys, at_y, lambda v, i, h=h: part.at[h, v * 4 + p_zh[i]], p_sent[h], y_in)
        for h in range(2)
    ]
    pz = [new("recv") for _ in range(2)]

    def partial_place(h, i):
        for v in ys + (y,):
            t = v * 4 + p_zh[i]
            part[h, t] = bf16(chain[last_f[t]])

    def partial_total(h):
        for i in range(4):
            mid[h, i] = p_ring[h].total(i, part[h, y * 4 + p_zh[i]])
            if i < 3:
                send(mid.at[h, i], zh_in.at[h, i], at_zh(p_zh[i]), p_sent[h], pz[h])

    feature_half(0)
    tiles_in.wait()
    products(0, tiles, slab, cols_s, prev_f)
    for i in range(4):
        partial_place(0, i)
        p_ring[0].terms(i)
    feature_half(1)
    products(1, tiles, slab, cols_s, prev_f)
    for i in range(4):
        partial_place(1, i)
        p_ring[1].terms(i)
    def turn(k, carry):
        turned[k] = tiles[k].T
        return carry

    lax.fori_loop(0, SLOTS, turn, 0, unroll=4)
    partial_total(0)
    partial_total(1)
    chain_tables(cols_s, live, prev_b, last_b, TILE_COLS)
    for copy in dense_in:
        copy.wait()
    agg = []
    for h in range(2):
        arrived(pz[h], zh_in.at[h])
        agg.append(bf16(f32(mid[h, 3]) + f32(zh_in[h, 0]) + f32(zh_in[h, 1]) + f32(zh_in[h, 2])))

    pre = bias[...] + jnp.dot(agg[0], wgt[0:COLS, :], preferred_element_type=jnp.float32)
    pre = pre + jnp.dot(agg[1], wgt[COLS:H, :], preferred_element_type=jnp.float32)
    cdf = 0.5 * (1.0 + lax.erf(pre * INV_SQRT2))
    slope = cdf + pre * (jnp.exp(-0.5 * pre * pre) * INV_SQRT_2PI)
    grad_pre = bf16(f32(cot[...]) * slope)
    grad_agg = bf16(
        lax.dot_general(grad_pre, wgt[...], (((1,), (1,)), ((), ())), preferred_element_type=jnp.float32)
    )

    g_sent = [new("send") for _ in range(2)]
    gz = [[new("recv") for _ in range(3)] for _ in range(2)]
    gy = [[new("recv") for _ in range(4)] for _ in range(2)]
    g_zh = (zh, zhs[0], zhs[2], zhs[1])

    def to_y(h, i):
        b = y * 4 + g_zh[i]
        for v in ys:
            send(gslab[h].at[b], gslab[h].at[b], at_y(v), g_sent[h], gy[h][i])

    def to_zh(h, i):
        send(gslab[h].at[col], gslab[h].at[col], at_zh(zhs[i]), g_sent[h], gz[h][i])

    for h in range(2):
        gslab[h][col] = grad_agg[:, COLS * h : COLS * h + COLS]
        if h == 0:
            for i in (1, 2, 0):
                to_zh(0, i)
        to_y(h, 0)
    hid[...] = bf16(pre * cdf)
    hid_out = local(hid, hidden_out)

    w_sent = [new("send") for _ in range(8)]
    w_recv = [new("recv") for _ in range(8)]
    both = jnp.concatenate(agg, axis=1)
    grad_w = lax.dot_general(both, grad_pre, (((0,), (0,)), ((), ())), preferred_element_type=jnp.float32)
    w0[0, 0:128] = grad_w[0:128]
    w0[1, 0:128] = grad_w[128:256]
    grad_b = jnp.broadcast_to(jnp.sum(f32(grad_pre), axis=0, keepdims=True), (8, H))
    w0[0, 128:136] = grad_b
    w0[1, 128:136] = grad_b
    send(w0.at[other], w0_in, sibling, w_sent[0], w_recv[0])

    def weight_x():
        arrived(w_recv[0], w0_in)
        s = w0[core] + w0_in[...]
        for v in range(4):
            w1[v, 0:32] = s[32 * v : 32 * v + 32]
            w1[v, 32:40] = s[128:136]
        w1_in[x] = w1[x]
        for v in xs:
            send(w1.at[v], w1_in.at[x], at_x(v), w_sent[1], w_recv[1])

    def weight_y():
        arrived(w_recv[1], w1_in.at[pl.ds(0, 3)])
        w2_in[y] = w1_in[0] + w1_in[1] + w1_in[2] + w1_in[3]
        for v in ys:
            send(w2_in.at[y], w2_in.at[y], at_y(v), w_sent[2], w_recv[2])

    def weight_zl():
        arrived(w_recv[2], w2_in.at[pl.ds(0, 3)])
        s = w2_in[0] + w2_in[1] + w2_in[2] + w2_in[3]
        for v in range(4):
            w3[v, 0:8] = s[8 * v : 8 * v + 8]
            w3[v, 8:16] = s[32:40]
        w3_in[zl] = w3[zl]
        for v in zls:
            send(w3.at[v], w3_in.at[zl], at_zl(v), w_sent[3], w_recv[3])

    def weight_zh():
        arrived(w_recv[3], w3_in.at[pl.ds(0, 3)])
        w4_in[zh] = w3_in[0] + w3_in[1] + w3_in[2] + w3_in[3]
        for v in zhs:
            send(w4_in.at[zh], w4_in.at[zh], at_zh(v), w_sent[4], w_recv[4])

    mine = core * 16 + x * 4 + zl

    def weight_back_zl():
        arrived(w_recv[4], w4_in.at[pl.ds(0, 3)])
        s = (w4_in[0] + w4_in[1] + w4_in[2] + w4_in[3]) * (1.0 / math.sqrt(NODES))
        bfin[...] = s[8:9]
        wfin[mine] = s[0:8]
        for v in zls:
            send(wfin.at[mine], wfin.at[mine], at_zl(v), w_sent[5], w_recv[5])
        return local(bfin, bias_out)

    def weight_back_x():
        arrived(w_recv[5], wfin.at[pl.ds(0, 3)])
        quarter = pl.ds(core * 16 + x * 4, 4)
        for v in xs:
            send(wfin.at[quarter], wfin.at[quarter], at_x(v), w_sent[6], w_recv[6])

    def weight_back_core():
        arrived(w_recv[6], wfin.at[pl.ds(0, 12)])
        half = pl.ds(core * 16, 16)
        send(wfin.at[half], wfin.at[half], sibling, w_sent[7], w_recv[7])

    def gradient_relay(h, i):
        arrived(gz[h][i], gslab[h].at[0])
        to_y(h, i + 1)

    b_sent = [new("send") for _ in range(2)]
    bc = [[new("recv") for _ in range(4)] for _ in range(2)]
    bz = [new("recv") for _ in range(2)]
    b_zl = zls + (zl,)
    b_ring = [
        Ring(h, xs, at_x, lambda v, i, h=h: xsum.at[h, v * 4 + b_zl[i]], b_sent[h], x_in)
        for h in range(2)
    ]

    def back_half(h):
        for i in range(4):
            arrived(gy[h][i], gslab[h].at[pl.ds(0, 3)])
        products(h, turned, gslab, rows_s, prev_b)
        for i in range(4):
            for v in xs + (x,):
                t = block_of(v, b_zl[i], other)
                back[h, t] = bf16(chain[last_b[t]])
            for v in xs + (x,):
                t = block_of(v, b_zl[i], other)
                send(back.at[h, t], core_in.at[h, v * 4 + b_zl[i]], sibling, b_sent[h], bc[h][i])
        for i in range(4):
            for v in xs + (x,):
                t = block_of(v, b_zl[i], core)
                back[h, t] = bf16(chain[last_b[t]])

    def core_total(h, i):
        arrived(bc[h][i], core_in.at[h, pl.ds(0, 4)])
        for v in xs + (x,):
            q = v * 4 + b_zl[i]
            xsum[h, q] = bf16(f32(back[h, block_of(v, b_zl[i], core)]) + f32(core_in[h, q]))

    def x_total(h, i):
        zl_out[h, i] = b_ring[h].total(i, xsum[h, x * 4 + b_zl[i]])
        if i < 3:
            send(zl_out.at[h, i], zl_in.at[h, i], at_zl(b_zl[i]), b_sent[h], bz[h])

    def z_total(h):
        arrived(bz[h], zl_in.at[h])
        s = f32(zl_out[h, 3]) + f32(zl_in[h, 0]) + f32(zl_in[h, 1]) + f32(zl_in[h, 2])
        fin[h] = bf16(s)
        return local(fin.at[h], features_out.at[:, lanes(h)])

    def core_half(h):
        for i in range(4):
            core_total(h, i)
            b_ring[h].terms(i)

    weight_x()
    weight_y()
    for i in (1, 2, 0):
        to_zh(1, i)
    for i in (1, 2, 0):
        gradient_relay(0, i)
    weight_zl()
    gradient_relay(1, 1)
    gradient_relay(1, 2)
    weight_zh()
    back_half(0)
    gradient_relay(1, 0)
    core_half(0)
    back_half(1)
    core_half(1)
    b_out = weight_back_zl()
    for i in range(4):
        x_total(0, i)
    weight_back_x()
    for i in range(4):
        x_total(1, i)
    outs = [z_total(0)]
    weight_back_core()
    outs.append(z_total(1))
    arrived(w_recv[7], wfin.at[pl.ds(0, 16)])
    outs += [local(wfin, weight_out), hid_out, b_out]
    for h in range(2):
        left(f_sent[h], slab[h].at[pl.ds(0, 31)])
        left(p_sent[h], part.at[h, pl.ds(0, 15)])
        left(g_sent[h], gslab[h].at[pl.ds(0, 15)])
        left(b_sent[h], back.at[h, pl.ds(0, 31)])
    left(w_sent[0], w0_in)
    left(w_sent[1], w1_in.at[pl.ds(0, 3)])
    left(w_sent[2], w2_in.at[pl.ds(0, 3)])
    left(w_sent[3], w3_in.at[pl.ds(0, 3)])
    left(w_sent[4], w4_in.at[pl.ds(0, 3)])
    left(w_sent[5], wfin.at[pl.ds(0, 3)])
    left(w_sent[6], wfin.at[pl.ds(0, 12)])
    left(w_sent[7], wfin.at[pl.ds(0, 16)])
    for copy in outs:
        copy.wait()
    assert counts == {"send": SENDS, "recv": RECVS, "local": LOCALS}, counts


def write_kernel(hidden, weight, bias, features, hidden_out, weight_out, bias_out, features_out, h, w, b, f, sems):
    trios = ((features, f, features_out), (weight, w, weight_out), (hidden, h, hidden_out), (bias, b, bias_out))
    reads = [pltpu.make_async_copy(src, held, sems.at[i]) for i, (src, held, _) in enumerate(trios)]
    writes = [pltpu.make_async_copy(held, dst, sems.at[4 + i]) for i, (_, held, dst) in enumerate(trios)]
    for copy in reads:
        copy.start()
    for read, write in zip(reads, writes):
        read.wait()
        write.start()
    for copy in writes:
        copy.wait()


def shards(features, adjacency, block_rows, block_cols, block_count, weight, bias_term, cotangent):
    half, single = jnp.bfloat16, jnp.float32
    vmem = pltpu.VMEM
    hbm = pl.BlockSpec(memory_space=pl.ANY)
    scratch = [
        vmem((SLOTS, BS, BS), half),
        vmem((SLOTS, BS, BS), half),
        vmem((H, H), half),
        vmem((1, H), single),
        vmem((BS, H), half),
        vmem((SLOTS + 1, BS, COLS), single),
        vmem((TILE_COLS, BS, COLS), half),
        vmem((TILE_COLS, BS, COLS), half),
        vmem((2, TILE_ROWS, BS, COLS), half),
        vmem((2, 4, 3, BS, COLS), half),
        vmem((2, 4, BS, COLS), half),
        vmem((2, 3, BS, COLS), half),
        vmem((TILE_ROWS, BS, COLS), half),
        vmem((TILE_ROWS, BS, COLS), half),
        vmem((2, TILE_COLS, BS, COLS), half),
        vmem((2, 16, BS, COLS), half),
        vmem((2, 16, BS, COLS), half),
        vmem((2, 4, 3, BS, COLS), half),
        vmem((2, 4, BS, COLS), half),
        vmem((2, 3, BS, COLS), half),
        vmem((BS, H), half),
        vmem((2, BS, COLS), half),
        vmem((2, 136, H), single),
        vmem((136, H), single),
        vmem((4, 40, H), single),
        vmem((4, 40, H), single),
        vmem((4, 40, H), single),
        vmem((4, 16, H), single),
        vmem((4, 16, H), single),
        vmem((4, 16, H), single),
        vmem((32, 8, H), single),
        vmem((1, H), single),
        pltpu.SMEM((SLOTS,), jnp.int32),
        pltpu.SMEM((SLOTS,), jnp.int32),
        pltpu.SMEM((1, 1), jnp.int32),
        pltpu.SMEM((SLOTS,), jnp.int32),
        pltpu.SMEM((TILE_ROWS,), jnp.int32),
        pltpu.SMEM((SLOTS,), jnp.int32),
        pltpu.SMEM((TILE_COLS,), jnp.int32),
        pltpu.SemaphoreType.DMA((LOCALS,)),
        pltpu.SemaphoreType.DMA((SENDS,)),
        pltpu.SemaphoreType.DMA((RECVS,)),
    ]
    shapes = (
        jax.ShapeDtypeStruct((BS, H), half),
        jax.ShapeDtypeStruct((32, 8, H), single),
        jax.ShapeDtypeStruct((1, H), single),
        jax.ShapeDtypeStruct((BS, H), half),
    )
    results = pl.pallas_call(
        layer_kernel,
        out_shape=shapes,
        in_specs=[hbm] * 8,
        out_specs=(hbm,) * 4,
        scratch_shapes=scratch,
        compiler_params=pltpu.CompilerParams(
            collective_id=0, has_side_effects=True, vmem_limit_bytes=60 * 1024 * 1024
        ),
        name="gcn_layer",
    )(
        features,
        adjacency.reshape(SLOTS, BS, BS),
        block_rows.reshape(SLOTS),
        block_cols.reshape(SLOTS),
        block_count,
        weight,
        bias_term.reshape(1, H),
        cotangent,
    )
    hidden, grad_weight, grad_bias, grad_features = pl.pallas_call(
        write_kernel,
        out_shape=shapes,
        in_specs=[hbm] * 4,
        out_specs=(hbm,) * 4,
        scratch_shapes=[vmem(v.shape, v.dtype) for v in shapes] + [pltpu.SemaphoreType.DMA((8,))],
        compiler_params=pltpu.CompilerParams(vmem_limit_bytes=60 * 1024 * 1024),
        name="write_results",
    )(*results)
    return hidden, grad_weight.reshape(H, H), grad_bias.reshape(H), grad_features


def solution(mesh):
    return jax.shard_map(
        shards,
        mesh=mesh,
        in_specs=(
            P(("col", "row"), None),
            P("row", "col", None, None, None),
            P("row", "col", None),
            P("row", "col", None),
            P("row", "col"),
            P(),
            P(),
            P(("row", "col"), None),
        ),
        out_specs=(P(("row", "col"), None), P(), P(), P(("col", "row"), None)),
        check_vma=False,
    )
```
